512 devices in a mesh: row: 64 (over x, y, core), col: 8 (over z).
Axes of the slice: x: 4, y: 8, z: 8, core: 2. Of those that a mesh axis runs over, the one named last changes fastest.
Arguments:
- tile_values: bfloat16 [65536, 128, 128], P(('row', 'col')), may hold values from 0 to 4000, as said below
- tile_rows: int32 [65536], P(('row', 'col')), may hold values from 0 to 3, as said below
- tile_cols: int32 [65536], P(('row', 'col')), may hold values from 0 to 63
- tile_count: int32 [512], P(('row', 'col')), may hold values from 32 to 128, as said below
- sketch: bfloat16 [256, 65536], P('row', 'col'), may hold values from -0.0234375 to 0.0234375
Outputs:
- embed_rows: float32 [32768, 256], P(('row', 'col'))
- gram: float32 [256, 256], replicated
The draws below stay inside these ranges and needn't reach their ends.
Inputs may be any that keep to these rules, and one draw needn't show every extreme that they name: `tile_rows`: within one device the used and unused slots name distinct tile positions. `tile_count`: some device uses all 128 slots. `tile_values`: Nonnegative.
All inputs are finite; a program needn't handle non-finite values.
Results may differ from the reference program's by a relative error of at most 0.0029.
Values may be sent and summed in bfloat16 or wider, within the bound.
A program may use at most 64 MiB of HBM per device.

```python
import jax
import jax.numpy as jnp
from jax import lax

TS = 128
K = 256
RT = 4
CT = 64
TILE_SLOT_COUNT = 128
NR = 32768
NC = 65536
N_ROW = 64
N_COL = 8
DEVICES = 512


def common_slots(key):
    keys = jax.random.split(key, DEVICES)
    return jax.vmap(lambda k: jax.random.permutation(k, RT * CT)[:TILE_SLOT_COUNT])(keys).reshape(-1)


def draw_tile_rows(key, part):
    slots = common_slots(key)
    return (slots // CT).astype(jnp.int32)


def draw_tile_cols(key, part):
    slots = common_slots(key)
    return (slots % CT).astype(jnp.int32)


def draw_tile_count(key, part):
    key = jax.random.fold_in(key, 7)
    first, second = jax.random.split(key)
    counts = jax.random.randint(first, (DEVICES,), TILE_SLOT_COUNT // 4, TILE_SLOT_COUNT // 2 + 1)
    full = jax.random.randint(second, (), 0, DEVICES)
    return jnp.where(jnp.arange(DEVICES) == full, TILE_SLOT_COUNT, counts).astype(jnp.int32)


def draw_tile_values(key, part):
    key = jax.random.fold_in(key, 11)
    power_term_mask, power_term_weight, power_term_scale = jax.random.split(key, 3)
    shape = (DEVICES * TILE_SLOT_COUNT, TS, TS)
    mask = jax.random.bernoulli(power_term_mask, 0.3, shape).astype(jnp.float32)
    processor_unit = jnp.arange(DEVICES * TILE_SLOT_COUNT) // TILE_SLOT_COUNT
    rpos = (processor_unit // N_COL).astype(jnp.float32) / max(N_ROW - 1, 1)
    cpos = (processor_unit % N_COL).astype(jnp.float32) / max(N_COL - 1, 1)
    factor = jnp.exp(jnp.log(3.0) * (rpos + cpos))
    tile_value_scale = jnp.exp(jax.random.uniform(power_term_scale, (DEVICES * TILE_SLOT_COUNT,), jnp.float32, jnp.log(0.05), jnp.log(20.0)))
    weight = jnp.exp(jax.random.uniform(power_term_weight, shape, jnp.float32, jnp.log(0.1), jnp.log(10.0)))
    scale = (tile_value_scale * factor)[:, None, None]
    return (mask * weight * scale).astype(jnp.bfloat16)


def block_levels(rng, shape, cuts, low, largest):
    level = 1.0
    for dim, parts in cuts:
        steps = jax.random.uniform(jax.random.fold_in(jax.random.fold_in(rng, 6), dim), (parts,), jnp.float32, low / len(cuts), largest / len(cuts))
        level = level * jnp.repeat(jnp.exp(steps), shape[dim] // parts).reshape((-1,) + (1,) * (len(shape) - 1 - dim))
    return level


def scatter_about(stream_key, shape, deviation, most, shards=(), kind=jnp.bfloat16):
    loudness = block_levels(stream_key, shape, shards, -0.22, 0.18) if shards else 1.0
    drawn = jax.random.normal(stream_key, shape, jnp.float32) * deviation * loudness
    return jnp.minimum(jnp.maximum(drawn, -most), most).astype(kind)


def setup_inputs(seed: int = 0) -> dict:
    arg_keys = jax.random.split(jax.random.key(seed), 6)
    return {
        "tile_values": draw_tile_values(jax.random.fold_in(arg_keys[5], 71), 0),
        "tile_rows": draw_tile_rows(jax.random.fold_in(arg_keys[5], 71), 0),
        "tile_cols": draw_tile_cols(jax.random.fold_in(arg_keys[5], 71), 0),
        "tile_count": draw_tile_count(jax.random.fold_in(arg_keys[5], 71), 0),
        "sketch": scatter_about(arg_keys[4], (K, NC), NC ** -0.5, 0.0234375, ((0, 64), (1, 8))),
    }


def reference(tile_values, tile_rows, tile_cols, tile_count, sketch):
    vals = tile_values.reshape(DEVICES, TILE_SLOT_COUNT, TS, TS)
    rows = tile_rows.reshape(DEVICES, TILE_SLOT_COUNT)
    cols = tile_cols.reshape(DEVICES, TILE_SLOT_COUNT)
    processor_unit = jnp.arange(DEVICES, dtype=jnp.int32)
    grow = (processor_unit // N_COL)[:, None] * RT + rows
    gcol = (processor_unit % N_COL)[:, None] * CT + cols
    valid = (jnp.arange(TILE_SLOT_COUNT, dtype=jnp.int32)[None, :] < tile_count[:, None]).astype(jnp.float32)
    row_terms = jnp.sum(vals, axis=3, dtype=jnp.float32) * valid[:, :, None]
    col_terms = jnp.sum(vals, axis=2, dtype=jnp.float32) * valid[:, :, None]
    row_deg = 1.0 + jax.ops.segment_sum(row_terms.reshape(-1, TS), grow.reshape(-1), NR // TS)
    col_deg = 1.0 + jax.ops.segment_sum(col_terms.reshape(-1, TS), gcol.reshape(-1), NC // TS)
    vol = jnp.sum(row_terms)
    sketch3 = sketch.reshape(K, NC // TS, TS)

    def step(acc, index):
        value = vals[index].astype(jnp.float32)
        rglob = grow[index]
        cglob = gcol[index]
        ratio = vol * value / (row_deg[rglob][:, :, None] * col_deg[cglob][:, None, :])
        logm = (jnp.log(jnp.maximum(ratio, 1.0)) * valid[index][:, None, None]).astype(jnp.bfloat16)
        picked = jnp.take(sketch3, cglob, axis=1)
        contrib = jnp.einsum("tij,ktj->tik", logm.astype(jnp.float32), picked.astype(jnp.float32))
        return acc.at[rglob].add(contrib), None

    start = jnp.zeros((NR // TS, TS, K), jnp.float32)
    acc, unused = lax.scan(step, start, processor_unit)
    embed_rows = acc.reshape(NR, K)
    gram = jnp.dot(embed_rows.T, embed_rows, precision=lax.Precision.HIGHEST, preferred_element_type=jnp.float32) / NR
    return embed_rows, gram
```

```python
import jax
import jax.numpy as jnp
from jax import lax
from jax.experimental import pallas as pl
from jax.experimental.pallas import tpu as pltpu
from jax.sharding import PartitionSpec as P

MESH = pl.DeviceIdType.MESH
F32 = jnp.float32
BF16 = jnp.bfloat16

TS = 128
RT = 4
CT = 64
SLOTS = 128
K = 256
X, Y, Z = 4, 8, 8
U = 2 * X
ROW = X * Y * 2
NR = ROW * RT * TS
OWN = RT * TS
SHARE = OWN // Z
KROWS = 4
NT_DIMS = (((1,), (1,)), ((), ()))


def wrap(value, n):
    return lax.rem(value + 4 * n, n)


def each(n, f):
    def step(m, carry):
        f(m)
        return carry

    lax.fori_loop(1, n, step, 0)


def kernel(
    rows_v,
    cols_v,
    rows_s,
    cols_s,
    count_s,
    sketch,
    tiles,
    embed,
    gram,
    a,
    logm,
    gath,
    weights,
    acc,
    xf,
    inv_v,
    inv_s,
    colpart,
    colsrc,
    ycol,
    rowbuf,
    zrow,
    xdeg,
    ydeg,
    rscale,
    cinv,
    psend,
    precv,
    gsrc,
    gz,
    g64,
    gy,
    gx,
    gfull,
    gfin,
    tile_sem,
    inv_sem,
    ag_send,
    ag_recv,
    small_send,
    small_recv,
):
    row = lax.axis_index("row")
    z = lax.axis_index("col")
    core = lax.rem(row, 2)
    y = lax.rem(row // 2, Y)
    x = row // (2 * Y)
    u = 2 * x + core

    def y_peer(m):
        return wrap(y + m, Y)

    def u_peer(m):
        return wrap(u + m, U)

    def z_peer(m):
        return wrap(z + m, Z)

    def y_device(v):
        return ((x * Y + v) * 2 + core, z)

    def u_device(v):
        return ((v // 2 * Y + y) * 2 + lax.rem(v, 2), z)

    def z_device(v):
        return (row, v)

    part = SLOTS // 4
    tile_copies = [
        pltpu.make_async_copy(
            tiles.at[pl.ds(part * i, part)], a.at[pl.ds(part * i, part)], tile_sem.at[i]
        )
        for i in range(4)
    ]
    for copy in tile_copies:
        copy.start()

    barrier = pltpu.get_barrier_semaphore()

    def greet(device):
        pl.semaphore_signal(barrier, inc=1, device_id=device, device_id_type=MESH)

    each(Y, lambda m: greet(y_device(y_peer(m))))
    each(U, lambda m: greet(u_device(u_peer(m))))
    each(Z, lambda m: greet(z_device(z_peer(m))))

    lane = lax.broadcasted_iota(jnp.int32, (TS, TS), 1)
    sub = lax.broadcasted_iota(jnp.int32, (TS, TS), 0)
    pos = rows_v[...] * CT + cols_v[...]
    pos = jnp.where(lane[:1] < count_s[0], pos, -1)
    pos_t = jnp.broadcast_to(pos, (TS, TS)).T
    inv_v[...] = jnp.full((8, TS), SLOTS, jnp.int32)
    for h in range(2):
        hit = pos_t == lane + TS * h
        inv_v[pl.ds(h, 1), :] = SLOTS + jnp.sum(
            jnp.where(hit, sub - SLOTS, 0), axis=0, keepdims=True
        )
    inv_copy = pltpu.make_async_copy(inv_v, inv_s, inv_sem)
    inv_copy.start()

    def slot_at(r, c):
        return inv_s[r // 2, (r % 2) * CT + c]

    own = sketch[...].astype(F32)
    xf[pl.ds(0, KROWS), :] = own
    xf[pl.ds(KROWS, KROWS), :] = own
    low = lax.broadcasted_iota(jnp.int32, (8, TS), 0) < KROWS
    for cc in range(CT // 4):
        pieces = [xf[:, pl.ds(TS * (4 * cc + i), TS)] for i in range(4)]
        block = jnp.concatenate(
            [jnp.where(low, pieces[0], pieces[1]), jnp.where(low, pieces[2], pieces[3])], axis=0
        )
        gath[row, pl.ds(16 * cc, 16), :] = block.astype(BF16)

    pl.semaphore_wait(barrier, Y + U + Z - 3)

    def block_copy(d, target):
        return pltpu.make_async_remote_copy(
            src_ref=gath.at[d],
            dst_ref=gath.at[d],
            send_sem=ag_send,
            recv_sem=ag_recv.at[d],
            device_id=(target, z),
            device_id_type=MESH,
        )

    def sibling_send(d):
        block_copy(d, row + 1 - 2 * core).start()

    def arrived(d):
        block_copy(d, row + 1 - 2 * core).wait_recv()

    def hops(n, way):
        return n // 2 if way > 0 else n // 2 - 1

    def plan(which):
        if which == 0:
            n_p, n_s, a_p, a_s = X, Y, x, y

            def rid(p, s):
                return (p * Y + s) * 2
        else:
            n_p, n_s, a_p, a_s = Y, X, y, x

            def rid(p, s):
                return (s * Y + p) * 2 + 1

        sign_p = 1 - 2 * lax.rem(a_s, 2)

        def origin_p(way, dist):
            return wrap(a_p - way * sign_p * dist, n_p)

        def p_target(way):
            return rid(wrap(a_p + way * sign_p, n_p), a_s)

        def s_target(sign_s, way):
            return rid(a_p, wrap(a_s + way * sign_s, n_s))

        def first(o_p, d, onward):
            for way in onward:
                block_copy(d, p_target(way)).start()
            sign_s = 1 - 2 * lax.rem(o_p, 2)
            for way in (1, -1):
                if hops(n_s, way) >= 1:
                    block_copy(d, s_target(sign_s, way)).start()
            sibling_send(d)

        def start():
            first(a_p, row, [way for way in (1, -1) if hops(n_p, way) >= 1])

        def wave(t):
            sources = [(1, 0)]
            for way in (1, -1):
                for dist in range(1, hops(n_p, way) + 1):
                    sources.append((way, dist))
                    if dist == t:
                        o_p = origin_p(way, dist)
                        d = rid(o_p, a_s)
                        arrived(d)
                        first(o_p, d, [way] if dist < hops(n_p, way) else [])
            for way_p, dist_p in sources:
                dist = t - dist_p
                for way in (1, -1):
                    if not 1 <= dist <= hops(n_s, way):
                        continue
                    o_p = origin_p(way_p, dist_p)
                    sign_s = 1 - 2 * lax.rem(o_p, 2)
                    d = rid(o_p, wrap(a_s - way * sign_s * dist, n_s))
                    arrived(d)
                    if dist < hops(n_s, way):
                        block_copy(d, s_target(sign_s, way)).start()
                    sibling_send(d)

        return start, wave

    def gather_step(t):
        for which in (0, 1):

            @pl.when(core == which)
            def _(which=which):
                start, wave = plan(which)
                if t == 0:
                    start()
                else:
                    wave(t)

    gather_step(0)

    a[SLOTS] = jnp.zeros((TS, TS), BF16)
    logm[SLOTS] = jnp.zeros((TS, TS), BF16)
    inv_copy.wait()
    for copy in tile_copies:
        copy.wait()
    rowbuf[...] = jnp.zeros((8, TS), F32)
    for r in range(RT):

        def add(c, total, r=r):
            tile = a[slot_at(r, c)].astype(F32)
            columns = jnp.sum(tile.reshape(TS // 8, 8, TS), axis=0)
            if r == 0:
                colpart[c] = columns
            else:
                colpart[c] += columns
            return total + tile

        total = lax.fori_loop(0, CT, add, jnp.zeros((TS, TS), F32))
        rowbuf[pl.ds(r, 1), :] = jnp.sum(total.T, axis=0, keepdims=True)
    colsrc[...] = jnp.sum(colpart[...], axis=1).reshape(Y, CT // Y, TS)

    def small(phase, slot, src, dst, device):
        return pltpu.make_async_remote_copy(
            src_ref=src,
            dst_ref=dst,
            send_sem=small_send.at[phase],
            recv_sem=small_recv.at[phase, slot],
            device_id=device,
            device_id_type=MESH,
        )

    def send_y(phase, src, dst):
        each(Y, lambda m: small(phase, y, src(y_peer(m)), dst.at[y], y_device(y_peer(m))).start())

    def send_u(phase, src, dst):
        each(U, lambda m: small(phase, u, src(u_peer(m)), dst.at[u], u_device(u_peer(m))).start())

    def send_z(phase, src, dst):
        each(Z, lambda m: small(phase, z, src(z_peer(m)), dst.at[z], z_device(z_peer(m))).start())

    def recv_y(phase, dst):
        each(Y, lambda m: small(phase, y_peer(m), dst.at[y_peer(m)], dst.at[y_peer(m)], y_device(y_peer(m))).wait_recv())

    def recv_u(phase, dst):
        each(U, lambda m: small(phase, u_peer(m), dst.at[u_peer(m)], dst.at[u_peer(m)], u_device(u_peer(m))).wait_recv())

    def recv_z(phase, dst):
        each(Z, lambda m: small(phase, z_peer(m), dst.at[z_peer(m)], dst.at[z_peer(m)], z_device(z_peer(m))).wait_recv())

    def sent(phase, dst):
        view = dst.at[pl.ds(0, 7)]
        small(phase, 0, view, view, z_device(z_peer(1))).wait_send()

    send_z(0, lambda v: rowbuf, zrow)
    send_y(1, lambda v: colsrc.at[v], ycol)
    zrow[z] = rowbuf[...]
    ycol[y] = colsrc[y]
    gather_step(1)
    recv_z(0, zrow)
    recv_y(1, ycol)
    row_sum = jnp.sum(zrow[...], axis=0)
    xdeg[u, pl.ds(0, 8), :] = jnp.sum(ycol[...], axis=0)
    xdeg[u, pl.ds(8, 8), :] = jnp.broadcast_to(jnp.sum(row_sum), (8, TS))
    send_u(2, lambda v: xdeg.at[u], xdeg)
    gather_step(2)
    recv_u(2, xdeg)
    ydeg[y] = jnp.sum(xdeg[...], axis=0)
    send_y(3, lambda v: ydeg.at[y], ydeg)
    gather_step(3)
    recv_y(3, ydeg)
    cinv[...] = 1.0 / (1.0 + ydeg[:, pl.ds(0, 8), :].reshape(CT, TS))
    volume = jnp.sum(ydeg[:, pl.ds(8, 8), :], axis=0)
    scale = volume / (1.0 + row_sum)
    for r in range(RT):
        rscale[r] = jnp.broadcast_to(scale[r : r + 1], (TS, TS)).T

    def log_step(s, carry):
        tile = a[s].astype(F32)
        ratio = tile * rscale[rows_s[s]] * cinv[pl.ds(cols_s[s], 1), :]
        logm[s] = jnp.log(jnp.maximum(ratio, 1.0)).astype(BF16)
        return carry

    lax.fori_loop(0, SLOTS // 2, log_step, 0)
    gather_step(4)
    lax.fori_loop(SLOTS // 2, SLOTS, log_step, 0)
    gather_step(5)
    gather_step(6)

    def from_sibling(i, carry):
        arrived(2 * i + 1 - core)
        return carry

    lax.fori_loop(0, ROW // 2, from_sibling, 0)

    def quad(i, carry):
        q, cc = i // (CT // 4), lax.rem(i, CT // 4)
        start = pl.multiple_of(16 * cc, 16)
        parts = [gath[4 * q + j, pl.ds(start, 16), :].astype(F32) for j in range(4)]
        for half in range(2):
            f = [p[8 * half : 8 * half + 8] for p in parts]
            g = [pltpu.roll(v, 4, 0) for v in f]
            first = [jnp.where(low, f[0], g[1]), jnp.where(low, f[2], g[3])]
            second = [jnp.where(low, g[0], f[1]), jnp.where(low, g[2], f[3])]
            for j, pair in enumerate((first, second)):
                weights[4 * cc + 2 * half + j, pl.ds(pl.multiple_of(16 * q, 16), 16), :] = (
                    jnp.concatenate(pair, axis=0).astype(BF16)
                )
        return carry

    lax.fori_loop(0, ROW // 4 * (CT // 4), quad, 0)

    acc[...] = jnp.zeros((OWN, K), F32)

    def product(i, carry):
        right = jnp.concatenate([weights[2 * i], weights[2 * i + 1]], axis=1)
        for r in range(RT):
            left = jnp.concatenate(
                [logm[slot_at(r, 2 * i)], logm[slot_at(r, 2 * i + 1)]], axis=1
            )
            acc[pl.ds(TS * r, TS), :] += lax.dot_general(
                left, right, NT_DIMS, preferred_element_type=F32
            )
        return carry

    lax.fori_loop(0, CT // 2, product, 0)

    psend[...] = acc[...].reshape(Z, SHARE, K).astype(BF16)
    send_z(4, lambda v: psend.at[v], precv)
    precv[z] = jnp.zeros((SHARE, K), BF16)
    recv_z(4, precv)
    result = acc[pl.ds(pl.multiple_of(z * SHARE, SHARE), SHARE), :]
    for i in range(Z):
        result = result + precv[i].astype(F32)
    embed[...] = result

    local_gram = lax.dot_general(
        result,
        result,
        (((0,), (0,)), ((), ())),
        precision=lax.Precision.HIGHEST,
        preferred_element_type=F32,
    ) * (1.0 / NR)
    gsrc[...] = local_gram.reshape(Z, K // Z, K)
    send_z(5, lambda v: gsrc.at[v], gz)
    gz[z] = gsrc[z]
    recv_z(5, gz)
    mine = jnp.sum(gz[...], axis=0)
    g64[pl.ds(0, 4)] = mine[:, :TS].reshape(4, 8, TS)
    g64[pl.ds(4, 4)] = mine[:, TS:].reshape(4, 8, TS)
    send_y(6, lambda v: g64.at[v], gy)
    gy[y] = g64[y]
    recv_y(6, gy)
    gx[u] = jnp.sum(gy[...], axis=0)
    send_u(7, lambda v: gx.at[u], gx)
    recv_u(7, gx)
    gfull[y] = jnp.sum(gx[...], axis=0)
    send_y(8, lambda v: gfull.at[y], gfull)
    recv_y(8, gfull)
    send_z(9, lambda v: gfull, gfin)
    gfin[z] = gfull[...]
    recv_z(9, gfin)
    for i in range(Z):
        gram[pl.ds(32 * i, 32), pl.ds(0, TS)] = gfin[i, pl.ds(0, 4)].reshape(32, TS)
        gram[pl.ds(32 * i, 32), pl.ds(TS, TS)] = gfin[i, pl.ds(4, 4)].reshape(32, TS)

    sent(0, zrow)
    sent(1, ycol)
    sent(2, xdeg)
    sent(3, ydeg)
    sent(4, precv)
    sent(5, gz)
    sent(6, gy)
    sent(7, gx)
    sent(8, gfull)
    sent(9, gfin)
    gone = gath.at[pl.ds(0, ROW - 1)]
    pltpu.make_async_remote_copy(
        src_ref=gone,
        dst_ref=gone,
        send_sem=ag_send,
        recv_sem=ag_recv.at[0],
        device_id=(row + 1 - 2 * core, z),
        device_id_type=MESH,
    ).wait_send()


def local(tile_values, tile_rows, tile_cols, tile_count, sketch):
    vmem = pl.BlockSpec(memory_space=pltpu.VMEM)
    smem = pl.BlockSpec(memory_space=pltpu.SMEM)
    scratch = [
        pltpu.VMEM((SLOTS + 1, TS, TS), BF16),
        pltpu.VMEM((SLOTS + 1, TS, TS), BF16),
        pltpu.VMEM((ROW, CT * KROWS, TS), BF16),
        pltpu.VMEM((CT, K, TS), BF16),
        pltpu.VMEM((OWN, K), F32),
        pltpu.VMEM((8, CT * TS), F32),
        pltpu.VMEM((8, TS), jnp.int32),
        pltpu.SMEM((8, TS), jnp.int32),
        pltpu.VMEM((CT, 8, TS), F32),
        pltpu.VMEM((Y, CT // Y, TS), F32),
        pltpu.VMEM((Y, 8, TS), F32),
        pltpu.VMEM((8, TS), F32),
        pltpu.VMEM((Z, 8, TS), F32),
        pltpu.VMEM((U, 16, TS), F32),
        pltpu.VMEM((Y, 16, TS), F32),
        pltpu.VMEM((RT, TS, TS), F32),
        pltpu.VMEM((CT, TS), F32),
        pltpu.VMEM((Z, SHARE, K), BF16),
        pltpu.VMEM((Z, SHARE, K), BF16),
        pltpu.VMEM((Z, K // Z, K), F32),
        pltpu.VMEM((Z, K // Z, K), F32),
        pltpu.VMEM((Y, 8, TS), F32),
        pltpu.VMEM((Y, 8, TS), F32),
        pltpu.VMEM((U, 8, TS), F32),
        pltpu.VMEM((Y, 8, TS), F32),
        pltpu.VMEM((Z, Y, 8, TS), F32),
        pltpu.SemaphoreType.DMA((4,)),
        pltpu.SemaphoreType.DMA,
        pltpu.SemaphoreType.DMA,
        pltpu.SemaphoreType.DMA((ROW,)),
        pltpu.SemaphoreType.DMA((10,)),
        pltpu.SemaphoreType.DMA((10, 8)),
    ]
    return pl.pallas_call(
        kernel,
        out_shape=(
            jax.ShapeDtypeStruct((SHARE, K), F32),
            jax.ShapeDtypeStruct((K, K), F32),
        ),
        in_specs=[vmem, vmem, smem, smem, smem, vmem, pl.BlockSpec(memory_space=pl.ANY)],
        out_specs=(vmem, vmem),
        scratch_shapes=scratch,
        compiler_params=pltpu.CompilerParams(
            collective_id=0, has_side_effects=True, vmem_limit_bytes=48 * 1024 * 1024
        ),
    )(
        tile_rows.reshape(1, SLOTS),
        tile_cols.reshape(1, SLOTS),
        tile_rows,
        tile_cols,
        tile_count,
        sketch,
        tile_values,
    )


def solution(mesh):
    placed = (
        P(("row", "col"), None, None),
        P(("row", "col")),
        P(("row", "col")),
        P(("row", "col")),
        P("row", "col"),
    )
    return jax.shard_map(
        local, mesh=mesh, in_specs=placed, out_specs=(P(("row", "col"), None), P()), check_vma=False
    )
```

```python
import jax
import jax.numpy as jnp
from jax import lax
from jax.experimental import pallas as pl
from jax.experimental.pallas import tpu as pltpu
from jax.sharding import PartitionSpec as P

MESH = pl.DeviceIdType.MESH
F32 = jnp.float32
BF16 = jnp.bfloat16

TS = 128
RT = 4
CT = 64
SLOTS = 128
K = 256
X, Y, Z = 4, 8, 8
U = 2 * X
ROW = X * Y * 2
NR = ROW * RT * TS
OWN = RT * TS
SHARE = OWN // Z
KROWS = 4
H = 64
GROWS = 5 * H // U
NT_DIMS = (((1,), (1,)), ((), ()))


def wrap(value, n):
    return lax.rem(value + 4 * n, n)


def each(n, f):
    def step(m, carry):
        f(m)
        return carry

    lax.fori_loop(1, n, step, 0)


def kernel(
    rows_h,
    cols_h,
    count_h,
    sketch_h,
    tiles,
    embed,
    gram,
    a,
    logm,
    gath,
    weights,
    acc,
    sketch,
    xf,
    rows_v,
    cols_v,
    rows_s,
    cols_s,
    count_s,
    inv_v,
    inv_s,
    colpart,
    colsrc,
    ucol,
    rowbuf,
    zrow,
    ydeg,
    udeg,
    rscale,
    cinv,
    psend,
    precv,
    gsrc,
    gu,
    gy,
    gz,
    gfin,
    tile_sem,
    in_sem,
    inv_sem,
    ag_send,
    ag_recv,
    small_send,
    small_recv,
):
    row = lax.axis_index("row")
    z = lax.axis_index("col")
    core = lax.rem(row, 2)
    y = lax.rem(row // 2, Y)
    x = row // (2 * Y)
    u = 2 * x + core

    def y_peer(m):
        return wrap(y + m, Y)

    def u_peer(m):
        return wrap(u + m, U)

    def z_peer(m):
        return wrap(z + m, Z)

    def rid(xx, yy):
        return (xx * Y + yy) * 2 + core

    def y_device(v):
        return (rid(x, v), z)

    def u_device(v):
        return ((v // 2 * Y + y) * 2 + lax.rem(v, 2), z)

    def z_device(v):
        return (row, v)

    barrier = pltpu.get_barrier_semaphore()

    def greet(device):
        pl.semaphore_signal(barrier, inc=1, device_id=device, device_id_type=MESH)

    each(Y, lambda m: greet(y_device(y_peer(m))))
    each(U, lambda m: greet(u_device(u_peer(m))))
    each(Z, lambda m: greet(z_device(z_peer(m))))

    in_copies = [
        pltpu.make_async_copy(src, dst, in_sem.at[i])
        for i, (src, dst) in enumerate(
            (
                (sketch_h, sketch),
                (rows_h, rows_v),
                (cols_h, cols_v),
                (count_h, count_s),
                (rows_h, rows_s),
                (cols_h, cols_s),
            )
        )
    ]
    for copy in in_copies:
        copy.start()
    part = SLOTS // 4
    tile_copies = [
        pltpu.make_async_copy(
            tiles.at[pl.ds(part * i, part)], a.at[pl.ds(part * i, part)], tile_sem.at[i]
        )
        for i in range(4)
    ]
    for copy in tile_copies:
        copy.start()

    in_copies[0].wait()
    own = sketch[...].astype(F32)
    xf[pl.ds(0, KROWS), :] = own
    xf[pl.ds(KROWS, KROWS), :] = own
    low = lax.broadcasted_iota(jnp.int32, (8, TS), 0) < KROWS
    for cc in range(CT // 4):
        pieces = [xf[:, pl.ds(TS * (4 * cc + i), TS)] for i in range(4)]
        block = jnp.concatenate(
            [jnp.where(low, pieces[0], pieces[1]), jnp.where(low, pieces[2], pieces[3])], axis=0
        )
        gath[row, pl.ds(16 * cc, 16), :] = block.astype(BF16)

    for copy in in_copies[1:]:
        copy.wait()
    lane = lax.broadcasted_iota(jnp.int32, (TS, TS), 1)
    sub = lax.broadcasted_iota(jnp.int32, (TS, TS), 0)
    pos = rows_v[...] * CT + cols_v[...]
    pos = jnp.where(lane[:1] < count_s[0], pos, -1)
    pos_t = jnp.broadcast_to(pos, (TS, TS)).T
    inv_v[...] = jnp.full((8, TS), SLOTS, jnp.int32)
    for h in range(2):
        hit = pos_t == lane + TS * h
        inv_v[pl.ds(h, 1), :] = SLOTS + jnp.sum(
            jnp.where(hit, sub - SLOTS, 0), axis=0, keepdims=True
        )
    inv_copy = pltpu.make_async_copy(inv_v, inv_s, inv_sem)
    inv_copy.start()

    def slot_at(r, c):
        return inv_s[r // 2, (r % 2) * CT + c]

    pl.semaphore_wait(barrier, Y + U + Z - 3)

    def block_copy(d, target):
        return pltpu.make_async_remote_copy(
            src_ref=gath.at[d],
            dst_ref=gath.at[d],
            send_sem=ag_send,
            recv_sem=ag_recv.at[d],
            device_id=(target, z),
            device_id_type=MESH,
        )

    sibling = row + 1 - 2 * core

    def arrived(d):
        block_copy(d, sibling).wait_recv()

    def along_x(d):
        block_copy(d, rid(wrap(x + 1, X), y)).start()
        block_copy(d, rid(wrap(x - 1, X), y)).start()

    def to_sibling(d):
        block_copy(d, sibling).start()

    def near(m):
        yy = y_peer(m)
        sign = 1 - 2 * lax.rem(yy, 2)
        relayed = rid(wrap(x - sign, X), yy)
        other = rid(wrap(x + sign, X), yy)
        arrived(relayed)
        block_copy(relayed, rid(wrap(x + sign, X), y)).start()
        to_sibling(relayed)
        arrived(other)
        to_sibling(other)

    def far(m):
        d = rid(wrap(x + 2, X), y_peer(m))
        arrived(d)
        to_sibling(d)

    def by_y(m):
        d = rid(x, y_peer(m))
        arrived(d)
        along_x(d)
        if m not in (-3, 4):
            block_copy(d, rid(x, y_peer(-1 if m > 0 else 1))).start()
        to_sibling(d)

    rings = ((0,), (1, -1), (2, -2), (3, -3), (4,))

    def gather_step(t):
        if t == 0:
            along_x(row)
            for m in (1, -1):
                block_copy(row, rid(x, y_peer(m))).start()
            to_sibling(row)
            return
        for f, i in ((by_y, t), (near, t - 1), (far, t - 2)):
            if 0 <= i < len(rings):
                for m in rings[i]:
                    if f is not by_y or m != 0:
                        f(m)

    gather_step(0)

    a[SLOTS] = jnp.zeros((TS, TS), BF16)
    logm[SLOTS] = jnp.zeros((TS, TS), BF16)
    inv_copy.wait()
    for copy in tile_copies:
        copy.wait()
    rowbuf[...] = jnp.zeros((8, TS), F32)
    for r in range(RT):

        def add(c, total, r=r):
            tile = a[slot_at(r, c)].astype(F32)
            columns = jnp.sum(tile.reshape(TS // 8, 8, TS), axis=0)
            if r == 0:
                colpart[c] = columns
            else:
                colpart[c] += columns
            return total + tile

        total = lax.fori_loop(0, CT, add, jnp.zeros((TS, TS), F32), unroll=8)
        rowbuf[pl.ds(r, 1), :] = jnp.sum(total.T, axis=0, keepdims=True)
    colsrc[...] = jnp.sum(colpart[...], axis=1).reshape(U, CT // U, TS)

    def small(phase, slot, src, dst, device):
        return pltpu.make_async_remote_copy(
            src_ref=src,
            dst_ref=dst,
            send_sem=small_send.at[phase],
            recv_sem=small_recv.at[phase, slot],
            device_id=device,
            device_id_type=MESH,
        )

    def send_y(phase, src, dst):
        each(Y, lambda m: small(phase, y, src(y_peer(m)), dst.at[y], y_device(y_peer(m))).start())

    def send_u(phase, src, dst):
        each(U, lambda m: small(phase, u, src(u_peer(m)), dst.at[u], u_device(u_peer(m))).start())

    def send_z(phase, src, dst):
        each(Z, lambda m: small(phase, z, src(z_peer(m)), dst.at[z], z_device(z_peer(m))).start())

    def recv_y(phase, dst):
        each(Y, lambda m: small(phase, y_peer(m), dst.at[y_peer(m)], dst.at[y_peer(m)], y_device(y_peer(m))).wait_recv())

    def recv_u(phase, dst):
        each(U, lambda m: small(phase, u_peer(m), dst.at[u_peer(m)], dst.at[u_peer(m)], u_device(u_peer(m))).wait_recv())

    def recv_z(phase, dst):
        each(Z, lambda m: small(phase, z_peer(m), dst.at[z_peer(m)], dst.at[z_peer(m)], z_device(z_peer(m))).wait_recv())

    def sent(phase, dst):
        view = dst.at[pl.ds(0, 7)]
        small(phase, 0, view, view, z_device(z_peer(1))).wait_send()

    send_z(0, lambda v: rowbuf, zrow)
    send_u(1, lambda v: colsrc.at[v], ucol)
    zrow[z] = rowbuf[...]
    ucol[u] = colsrc[u]
    gather_step(1)
    recv_u(1, ucol)
    recv_z(0, zrow)
    row_sum = jnp.sum(zrow[...], axis=0)
    ydeg[y, pl.ds(0, 8), :] = jnp.sum(ucol[...], axis=0)
    ydeg[y, pl.ds(8, 8), :] = row_sum
    send_y(2, lambda v: ydeg.at[y], ydeg)
    gather_step(2)
    recv_y(2, ydeg)
    udeg[u] = jnp.sum(ydeg[...], axis=0)
    send_u(3, lambda v: udeg.at[u], udeg)
    gather_step(3)
    recv_u(3, udeg)
    cinv[...] = 1.0 / (1.0 + udeg[:, pl.ds(0, 8), :].reshape(CT, TS))
    volume = jnp.sum(jnp.sum(udeg[:, pl.ds(8, 8), :], axis=0), axis=(0, 1), keepdims=True)
    scale = volume / (1.0 + row_sum)
    for r in range(RT):
        rscale[r] = jnp.broadcast_to(scale[r : r + 1], (TS, TS)).T

    def log_step(s, carry):
        tile = a[s].astype(F32)
        ratio = tile * rscale[rows_s[0, s]] * cinv[pl.ds(cols_s[0, s], 1), :]
        logm[s] = jnp.log(jnp.maximum(ratio, 1.0)).astype(BF16)
        return carry

    lax.fori_loop(0, SLOTS // 2, log_step, 0, unroll=4)
    gather_step(4)
    lax.fori_loop(SLOTS // 2, SLOTS, log_step, 0, unroll=4)

    def arrange(xx):
        def from_sibling(i, carry):
            arrived((xx * Y + i) * 2 + 1 - core)
            return carry

        lax.fori_loop(0, Y, from_sibling, 0)

        def quad(i, carry):
            q, cc = xx * (Y // 2) + i // (CT // 4), lax.rem(i, CT // 4)
            start = pl.multiple_of(16 * cc, 16)
            parts = [gath[4 * q + j, pl.ds(start, 16), :].astype(F32) for j in range(4)]
            for half in range(2):
                f = [p[8 * half : 8 * half + 8] for p in parts]
                g = [pltpu.roll(v, 4, 0) for v in f]
                first = [jnp.where(low, f[0], g[1]), jnp.where(low, f[2], g[3])]
                second = [jnp.where(low, g[0], f[1]), jnp.where(low, g[2], f[3])]
                for j, pair in enumerate((first, second)):
                    weights[4 * cc + 2 * half + j, pl.ds(pl.multiple_of(16 * q, 16), 16), :] = (
                        jnp.concatenate(pair, axis=0).astype(BF16)
                    )
            return carry

        lax.fori_loop(0, Y // 2 * (CT // 4), quad, 0, unroll=4)

    arrange(x)
    gather_step(5)
    arrange(wrap(x + 1, X))
    arrange(wrap(x - 1, X))
    gather_step(6)
    arrange(wrap(x + 2, X))

    depth = 16
    acc[...] = jnp.zeros((OWN, K), F32)
    for half in range(2):

        def product(i, carry, half=half):
            right = jnp.concatenate([weights[depth * i + t] for t in range(depth)], axis=1)
            left = jnp.concatenate(
                [
                    jnp.concatenate(
                        [logm[slot_at(r, depth * i + t)] for t in range(depth)], axis=1
                    )
                    for r in (2 * half, 2 * half + 1)
                ],
                axis=0,
            )
            acc[pl.ds(OWN // 2 * half, OWN // 2), :] += lax.dot_general(
                left, right, NT_DIMS, preferred_element_type=F32
            )
            return carry

        lax.fori_loop(0, CT // depth, product, 0)
        block = acc[pl.ds(OWN // 2 * half, OWN // 2), :]
        psend[pl.ds(Z // 2 * half, Z // 2)] = block.reshape(Z // 2, SHARE, K).astype(BF16)
        for i in range(Z // 2):
            v = Z // 2 * half + i

            @pl.when(z != v)
            def _(v=v):
                small(4, z, psend.at[v], precv.at[z], z_device(v)).start()

    precv[z] = jnp.zeros((SHARE, K), BF16)
    result = acc[pl.ds(pl.multiple_of(z * SHARE, SHARE), SHARE), :]
    recv_z(4, precv)
    for i in range(Z):
        result = result + precv[i].astype(F32)
    embed[...] = result

    local_gram = lax.dot_general(
        result,
        result,
        (((0,), (0,)), ((), ())),
        precision=lax.Precision.HIGHEST,
        preferred_element_type=F32,
    ) * (1.0 / NR)
    left = lax.broadcasted_iota(jnp.int32, (H, TS), 1) < H
    corner = jnp.where(
        left, pltpu.roll(local_gram[3 * H :, TS:], H, 1), local_gram[H : 2 * H, :TS]
    )
    gsrc[...] = jnp.concatenate(
        [local_gram[:H, :TS], local_gram[: 3 * H, TS:], corner], axis=0
    ).reshape(U, GROWS, TS)
    send_u(5, lambda v: gsrc.at[v], gu)
    gu[u] = gsrc[u]
    recv_u(5, gu)
    gy[y] = jnp.sum(gu[...], axis=0)
    send_y(6, lambda v: gy.at[y], gy)
    recv_y(6, gy)
    gz[z] = jnp.sum(gy[...], axis=0)
    send_z(7, lambda v: gz.at[z], gz)
    recv_z(7, gz)
    gfin[u] = jnp.sum(gz[...], axis=0)
    send_u(8, lambda v: gfin.at[u], gfin)
    recv_u(8, gfin)
    packed = gfin[...].reshape(5 * H, TS)
    corner = packed[4 * H :]
    mirrored = (lax.broadcasted_iota(jnp.int32, (TS, TS), 0) >= H) & (
        lax.broadcasted_iota(jnp.int32, (TS, TS), 1) < H
    )
    first = jnp.concatenate([packed[:H], corner], axis=0)
    gram[pl.ds(0, TS), pl.ds(0, TS)] = jnp.where(mirrored, first.T, first)
    across = packed[H : 3 * H]
    gram[pl.ds(0, TS), pl.ds(TS, TS)] = across
    gram[pl.ds(TS, TS), pl.ds(0, TS)] = across.T
    last = jnp.concatenate([packed[3 * H : 4 * H], pltpu.roll(corner, H, 1)], axis=0)
    gram[pl.ds(TS, TS), pl.ds(TS, TS)] = jnp.where(mirrored, last.T, last)

    sent(0, zrow)
    sent(1, ucol)
    sent(2, ydeg)
    sent(3, udeg)
    sent(4, precv)
    sent(5, gu)
    sent(6, gy)
    sent(7, gz)
    sent(8, gfin)
    gone = gath.at[pl.ds(0, ROW - 1)]
    pltpu.make_async_remote_copy(
        src_ref=gone,
        dst_ref=gone,
        send_sem=ag_send,
        recv_sem=ag_recv.at[0],
        device_id=(sibling, z),
        device_id_type=MESH,
    ).wait_send()


def hand_over(embed, gram, embed_out, gram_out):
    embed_out[...] = embed[...]
    gram_out[...] = gram[...]


def local(tile_values, tile_rows, tile_cols, tile_count, sketch):
    vmem = pl.BlockSpec(memory_space=pltpu.VMEM)
    hbm = pl.BlockSpec(memory_space=pltpu.HBM)
    scratch = [
        pltpu.VMEM((SLOTS + 1, TS, TS), BF16),
        pltpu.VMEM((SLOTS + 1, TS, TS), BF16),
        pltpu.VMEM((ROW, CT * KROWS, TS), BF16),
        pltpu.VMEM((CT, K, TS), BF16),
        pltpu.VMEM((OWN, K), F32),
        pltpu.VMEM((KROWS, CT * TS), BF16),
        pltpu.VMEM((8, CT * TS), F32),
        pltpu.VMEM((1, SLOTS), jnp.int32),
        pltpu.VMEM((1, SLOTS), jnp.int32),
        pltpu.SMEM((1, SLOTS), jnp.int32),
        pltpu.SMEM((1, SLOTS), jnp.int32),
        pltpu.SMEM((1,), jnp.int32),
        pltpu.VMEM((8, TS), jnp.int32),
        pltpu.SMEM((8, TS), jnp.int32),
        pltpu.VMEM((CT, 8, TS), F32),
        pltpu.VMEM((U, CT // U, TS), F32),
        pltpu.VMEM((U, 8, TS), F32),
        pltpu.VMEM((8, TS), F32),
        pltpu.VMEM((Z, 8, TS), F32),
        pltpu.VMEM((Y, 16, TS), F32),
        pltpu.VMEM((U, 16, TS), F32),
        pltpu.VMEM((RT, TS, TS), F32),
        pltpu.VMEM((CT, TS), F32),
        pltpu.VMEM((Z, SHARE, K), BF16),
        pltpu.VMEM((Z, SHARE, K), BF16),
        pltpu.VMEM((U, GROWS, TS), F32),
        pltpu.VMEM((U, GROWS, TS), F32),
        pltpu.VMEM((Y, GROWS, TS), F32),
        pltpu.VMEM((Z, GROWS, TS), F32),
        pltpu.VMEM((U, GROWS, TS), F32),
        pltpu.SemaphoreType.DMA((4,)),
        pltpu.SemaphoreType.DMA((6,)),
        pltpu.SemaphoreType.DMA,
        pltpu.SemaphoreType.DMA,
        pltpu.SemaphoreType.DMA((ROW,)),
        pltpu.SemaphoreType.DMA((9,)),
        pltpu.SemaphoreType.DMA((9, 8)),
    ]
    embed, gram = pl.pallas_call(
        kernel,
        out_shape=(
            jax.ShapeDtypeStruct((SHARE, K), F32),
            jax.ShapeDtypeStruct((K, K), F32),
        ),
        in_specs=[hbm] * 5,
        out_specs=(vmem, vmem),
        scratch_shapes=scratch,
        compiler_params=pltpu.CompilerParams(
            collective_id=0, has_side_effects=True, vmem_limit_bytes=63 * 1024 * 1024
        ),
    )(
        tile_rows.reshape(1, SLOTS),
        tile_cols.reshape(1, SLOTS),
        tile_count,
        sketch,
        tile_values,
    )
    return pl.pallas_call(
        hand_over,
        out_shape=(
            jax.ShapeDtypeStruct((SHARE, K), F32),
            jax.ShapeDtypeStruct((K, K), F32),
        ),
        in_specs=[vmem] * 2,
        out_specs=(vmem, vmem),
    )(embed, gram)


def solution(mesh):
    placed = (
        P(("row", "col"), None, None),
        P(("row", "col")),
        P(("row", "col")),
        P(("row", "col")),
        P("row", "col"),
    )
    return jax.shard_map(
        local, mesh=mesh, in_specs=placed, out_specs=(P(("row", "col"), None), P()), check_vma=False
    )
```

```python
import jax
import jax.numpy as jnp
from jax import lax
from jax.experimental import pallas as pl
from jax.experimental.pallas import tpu as pltpu
from jax.sharding import PartitionSpec as P

MESH = pl.DeviceIdType.MESH
F32 = jnp.float32
BF16 = jnp.bfloat16

TS = 128
RT = 4
CT = 64
SLOTS = 128
K = 256
X, Y, Z = 4, 8, 8
U = 2 * X
ROW = X * Y * 2
NR = ROW * RT * TS
OWN = RT * TS
SHARE = OWN // Z
KROWS = 4
GROWS = 3 * TS // U
NT_DIMS = (((1,), (1,)), ((), ()))


def wrap(value, n):
    return lax.rem(value + 4 * n, n)


def total_of(ref):
    total = ref[0].astype(F32)
    for i in range(1, ref.shape[0]):
        total = total + ref[i].astype(F32)
    return total


def each(n, f):
    def step(m, carry):
        f(m)
        return carry

    lax.fori_loop(1, n, step, 0, unroll=True)


def kernel(
    rows_h,
    cols_h,
    count_h,
    sketch_h,
    tiles,
    embed,
    gram,
    a,
    logm,
    gath,
    weights,
    acc,
    sketch,
    xf,
    rows_v,
    cols_v,
    rows_s,
    cols_s,
    count_s,
    inv_v,
    inv_s,
    colpart,
    colsrc,
    ucol,
    rowbuf,
    zrow,
    ydeg,
    udeg,
    rscale,
    cinv,
    psend,
    precv,
    gsrc,
    gu,
    gy,
    gz,
    gfin,
    tile_sem,
    in_sem,
    inv_sem,
    ag_send,
    sib_send,
    ag_recv,
    small_send,
    small_recv,
):
    row = lax.axis_index("row")
    z = lax.axis_index("col")
    core = lax.rem(row, 2)
    y = lax.rem(row // 2, Y)
    x = row // (2 * Y)
    u = 2 * x + core

    def y_peer(m):
        return wrap(y + m, Y)

    def u_peer(m):
        return wrap(u + m, U)

    def z_peer(m):
        return wrap(z + m, Z)

    def rid(xx, yy):
        return (xx * Y + yy) * 2 + core

    def y_device(v):
        return (rid(x, v), z)

    def u_device(v):
        return ((v // 2 * Y + y) * 2 + lax.rem(v, 2), z)

    def z_device(v):
        return (row, v)

    barrier = pltpu.get_barrier_semaphore()

    def greet(device):
        pl.semaphore_signal(barrier, inc=1, device_id=device, device_id_type=MESH)

    each(Y, lambda m: greet(y_device(y_peer(m))))
    each(U, lambda m: greet(u_device(u_peer(m))))
    each(Z, lambda m: greet(z_device(z_peer(m))))

    in_copies = [
        pltpu.make_async_copy(src, dst, in_sem.at[i])
        for i, (src, dst) in enumerate(
            (
                (sketch_h, sketch),
                (rows_h, rows_v),
                (cols_h, cols_v),
                (count_h, count_s),
                (rows_h, rows_s),
                (cols_h, cols_s),
            )
        )
    ]
    for copy in in_copies:
        copy.start()
    quarter = SLOTS // 4
    tile_copies = [
        pltpu.make_async_copy(
            tiles.at[pl.ds(quarter * i, quarter)],
            a.at[pl.ds(quarter * i, quarter)],
            tile_sem.at[i],
        )
        for i in range(4)
    ]
    for copy in tile_copies:
        copy.start()

    in_copies[0].wait()
    own = sketch[...].astype(F32)
    xf[pl.ds(0, KROWS), :] = own
    xf[pl.ds(KROWS, KROWS), :] = own
    low = lax.broadcasted_iota(jnp.int32, (8, TS), 0) < KROWS
    for cc in range(CT // 4):
        pieces = [xf[:, pl.ds(TS * (4 * cc + i), TS)] for i in range(4)]
        block = jnp.concatenate(
            [jnp.where(low, pieces[0], pieces[1]), jnp.where(low, pieces[2], pieces[3])], axis=0
        )
        gath[row, pl.ds(16 * cc, 16), :] = block.astype(BF16)

    for copy in in_copies[1:]:
        copy.wait()
    lane = lax.broadcasted_iota(jnp.int32, (TS, TS), 1)
    sub = lax.broadcasted_iota(jnp.int32, (TS, TS), 0)
    pos = rows_v[...] * CT + cols_v[...]
    pos = jnp.where(lane[:1] < count_s[0], pos, -1)
    pos_t = jnp.broadcast_to(pos, (TS, TS)).T
    inv_v[...] = jnp.full((8, TS), SLOTS, jnp.int32)
    for h in range(2):
        hit = pos_t == lane + TS * h
        inv_v[pl.ds(h, 1), :] = SLOTS + jnp.sum(
            jnp.where(hit, sub - SLOTS, 0), axis=0, keepdims=True
        )
    inv_copy = pltpu.make_async_copy(inv_v, inv_s, inv_sem)
    inv_copy.start()

    def slot_at(r, c):
        return inv_s[r // 2, (r % 2) * CT + c]


    a[SLOTS] = jnp.zeros((TS, TS), BF16)
    logm[SLOTS] = jnp.zeros((TS, TS), BF16)
    inv_copy.wait()
    for copy in tile_copies:
        copy.wait()
    rowbuf[...] = jnp.zeros((8, TS), F32)
    for r in range(RT):

        def add(c, total, r=r):
            tile = a[slot_at(r, c)].astype(F32)
            columns = jnp.sum(tile.reshape(TS // 8, 8, TS), axis=0)
            if r == 0:
                colpart[c] = columns
            else:
                colpart[c] += columns
            return total + tile

        total = lax.fori_loop(0, CT, add, jnp.zeros((TS, TS), F32), unroll=8)
        rowbuf[pl.ds(r, 1), :] = jnp.sum(total.T, axis=0, keepdims=True)
    colsrc[...] = jnp.sum(colpart[...], axis=1).reshape(U, CT // U, TS)

    pl.semaphore_wait(barrier, Y + U + Z - 3)

    sibling = row + 1 - 2 * core

    def block_copy(d, target):
        return pltpu.make_async_remote_copy(
            src_ref=gath.at[d],
            dst_ref=gath.at[d],
            send_sem=ag_send,
            recv_sem=ag_recv.at[d],
            device_id=(target, z),
            device_id_type=MESH,
        )

    def sibling_copy(d):
        return pltpu.make_async_remote_copy(
            src_ref=gath.at[d],
            dst_ref=gath.at[d],
            send_sem=sib_send,
            recv_sem=ag_recv.at[d],
            device_id=(sibling, z),
            device_id_type=MESH,
        )

    def arrived(d):
        sibling_copy(d).wait_recv()

    def to_sibling(d):
        sibling_copy(d).start()

    def along_x(d):
        block_copy(d, rid(wrap(x + 1, X), y)).start()
        block_copy(d, rid(wrap(x - 1, X), y)).start()

    def along_y(d, m):
        for way in (1, -1):
            if m == 0 or (way < 0 < m < Y // 2) or (way > 0 > m > 1 - Y // 2):
                block_copy(d, rid(x, y_peer(way))).start()

    def by_y(m):
        d = rid(x, y_peer(m))
        arrived(d)
        along_y(d, m)
        along_x(d)
        to_sibling(d)

    def near(m):
        yy = y_peer(m)
        sign = 1 - 2 * lax.rem(yy, 2)
        relayed = rid(wrap(x - sign, X), yy)
        other = rid(wrap(x + sign, X), yy)
        arrived(relayed)
        block_copy(relayed, rid(wrap(x + sign, X), y)).start()
        to_sibling(relayed)
        arrived(other)
        to_sibling(other)

    def far(m):
        d = rid(wrap(x + 2, X), y_peer(m))
        arrived(d)
        to_sibling(d)

    rings = ((0,), (1, -1), (2, -2), (3, -3), (4,))

    def gather_step(t):
        if t == 0:
            along_x(row)
            along_y(row, 0)
            to_sibling(row)
            return
        for f, i in ((by_y, t), (near, t - 1), (far, t - 2)):
            if 0 <= i < len(rings):
                for m in rings[i]:
                    if f is not by_y or m != 0:
                        f(m)


    def small(phase, slot, src, dst, device):
        return pltpu.make_async_remote_copy(
            src_ref=src,
            dst_ref=dst,
            send_sem=small_send.at[phase],
            recv_sem=small_recv.at[phase, slot],
            device_id=device,
            device_id_type=MESH,
        )

    def send_y(phase, src, dst):
        each(Y, lambda m: small(phase, y, src(y_peer(m)), dst.at[y], y_device(y_peer(m))).start())

    def send_u(phase, src, dst):
        each(U, lambda m: small(phase, u, src(u_peer(m)), dst.at[u], u_device(u_peer(m))).start())

    def send_z(phase, src, dst):
        each(Z, lambda m: small(phase, z, src(z_peer(m)), dst.at[z], z_device(z_peer(m))).start())

    def recv_y(phase, dst):
        each(Y, lambda m: small(phase, y_peer(m), dst.at[y_peer(m)], dst.at[y_peer(m)], y_device(y_peer(m))).wait_recv())

    def recv_u(phase, dst):
        each(U, lambda m: small(phase, u_peer(m), dst.at[u_peer(m)], dst.at[u_peer(m)], u_device(u_peer(m))).wait_recv())

    def recv_z(phase, dst):
        each(Z, lambda m: small(phase, z_peer(m), dst.at[z_peer(m)], dst.at[z_peer(m)], z_device(z_peer(m))).wait_recv())

    def sent(phase, dst):
        view = dst.at[pl.ds(0, 7)]
        small(phase, 0, view, view, z_device(z_peer(1))).wait_send()

    send_z(0, lambda v: rowbuf, zrow)
    send_u(1, lambda v: colsrc.at[v], ucol)
    gather_step(0)
    zrow[z] = rowbuf[...]
    ucol[u] = colsrc[u]
    gather_step(1)
    recv_u(1, ucol)
    recv_z(0, zrow)
    row_sum = jnp.sum(zrow[...], axis=0)
    ydeg[y, pl.ds(0, 8), :] = jnp.sum(ucol[...], axis=0)
    ydeg[y, pl.ds(8, 8), :] = row_sum
    send_y(2, lambda v: ydeg.at[y], ydeg)
    gather_step(2)
    recv_y(2, ydeg)
    udeg[u] = jnp.sum(ydeg[...], axis=0)
    send_u(3, lambda v: udeg.at[u], udeg)
    gather_step(3)
    recv_u(3, udeg)
    cinv[...] = 1.0 / (1.0 + udeg[:, pl.ds(0, 8), :].reshape(CT, TS))
    volume = jnp.sum(jnp.sum(udeg[:, pl.ds(8, 8), :], axis=0), axis=(0, 1), keepdims=True)
    scale = volume / (1.0 + row_sum)
    for r in range(RT):
        rscale[r] = jnp.broadcast_to(scale[r : r + 1], (TS, TS)).T

    def log_step(s, carry):
        tile = a[s].astype(F32)
        ratio = tile * rscale[rows_s[0, s]] * cinv[pl.ds(cols_s[0, s], 1), :]
        logm[s] = jnp.log(jnp.maximum(ratio, 1.0)).astype(BF16)
        return carry

    lax.fori_loop(0, SLOTS // 2, log_step, 0, unroll=4)
    gather_step(4)
    lax.fori_loop(SLOTS // 2, SLOTS, log_step, 0, unroll=4)

    def arrange(xx):
        def from_sibling(i, carry):
            arrived((xx * Y + i) * 2 + 1 - core)
            return carry

        lax.fori_loop(0, Y, from_sibling, 0)

        def quad(i, carry):
            q, cc = xx * (Y // 2) + i // (CT // 4), lax.rem(i, CT // 4)
            start = pl.multiple_of(16 * cc, 16)
            parts = [gath[4 * q + j, pl.ds(start, 16), :].astype(F32) for j in range(4)]
            for half in range(2):
                f = [p[8 * half : 8 * half + 8] for p in parts]
                g = [pltpu.roll(v, 4, 0) for v in f]
                first = [jnp.where(low, f[0], g[1]), jnp.where(low, f[2], g[3])]
                second = [jnp.where(low, g[0], f[1]), jnp.where(low, g[2], f[3])]
                for j, pair in enumerate((first, second)):
                    weights[4 * cc + 2 * half + j, pl.ds(pl.multiple_of(16 * q, 16), 16), :] = (
                        jnp.concatenate(pair, axis=0).astype(BF16)
                    )
            return carry

        lax.fori_loop(0, Y // 2 * (CT // 4), quad, 0, unroll=4)

    depth = 16
    mate = x + 1 - 2 * lax.rem(x, 2)
    acc[...] = jnp.zeros((2, OWN, TS), F32)

    def products(half, top):
        def product(i, carry):
            columns = pl.ds(pl.multiple_of(half * TS, TS), TS)
            right = jnp.concatenate(
                [weights[depth * i + t, columns, :] for t in range(depth)], axis=1
            )
            left = jnp.concatenate(
                [
                    jnp.concatenate(
                        [logm[slot_at(r, depth * i + t)] for t in range(depth)], axis=1
                    )
                    for r in (2 * top, 2 * top + 1)
                ],
                axis=0,
            )
            acc[half, pl.ds(OWN // 2 * top, OWN // 2), :] += lax.dot_general(
                left, right, NT_DIMS, preferred_element_type=F32
            )
            return carry

        lax.fori_loop(0, CT // depth, product, 0)
        psend[half, pl.ds(Z // 2 * top, Z // 2)] = (
            acc[half, pl.ds(OWN // 2 * top, OWN // 2), :]
            .reshape(Z // 2, SHARE, TS)
            .astype(BF16)
        )

    def scatter(phase, half, top):
        for i in range(Z // 2):
            v = Z // 2 * top + i

            @pl.when(z != v)
            def _(v=v):
                small(phase, z, psend.at[half, v], precv.at[half, z], z_device(v)).start()

    arrange(x)
    gather_step(5)
    arrange(mate)
    early = x // 2
    products(early, 0)
    scatter(4, early, 0)
    gather_step(6)
    products(early, 1)
    scatter(4, early, 1)
    arrange(wrap(x + 2, X))
    arrange(wrap(mate + 2, X))
    for top in range(2):
        products(1 - early, top)
        scatter(9, 1 - early, top)
    for half in range(2):
        precv[half, z] = jnp.zeros((SHARE, TS), BF16)
    recv_z(4, precv.at[early])
    recv_z(9, precv.at[1 - early])
    parts = []
    for half in range(2):
        part = acc[half, pl.ds(pl.multiple_of(z * SHARE, SHARE), SHARE), :]
        for i in range(Z):
            part = part + precv[half, i].astype(F32)
        embed[:, pl.ds(TS * half, TS)] = part
        parts.append(part)
    result = jnp.concatenate(parts, axis=1)

    local_gram = lax.dot_general(
        result,
        result,
        (((0,), (0,)), ((), ())),
        precision=lax.Precision.HIGHEST,
        preferred_element_type=F32,
    ) * (1.0 / NR)
    gsrc[...] = (
        jnp.concatenate([local_gram[:TS, :TS], local_gram[:, TS:]], axis=0)
        .reshape(U, GROWS, TS)
        .astype(BF16)
    )
    send_u(5, lambda v: gsrc.at[v], gu)
    gu[u] = gsrc[u]
    recv_u(5, gu)
    gy[y] = total_of(gu).astype(BF16)
    send_y(6, lambda v: gy.at[y], gy)
    recv_y(6, gy)
    gz[z] = total_of(gy).astype(BF16)
    send_z(7, lambda v: gz.at[z], gz)
    recv_z(7, gz)
    gfin[u] = total_of(gz)
    send_u(8, lambda v: gfin.at[u], gfin)
    recv_u(8, gfin)
    packed = gfin[...].reshape(3 * TS, TS)
    gram[pl.ds(0, TS), pl.ds(0, TS)] = packed[:TS]
    gram[:, pl.ds(TS, TS)] = packed[TS:]
    gram[pl.ds(TS, TS), pl.ds(0, TS)] = packed[TS : 2 * TS].T

    sent(0, zrow)
    sent(1, ucol)
    sent(2, ydeg)
    sent(3, udeg)
    sent(4, precv.at[0])
    sent(9, precv.at[1])
    sent(5, gu)
    sent(6, gy)
    sent(7, gz)
    sent(8, gfin)
    def gone(sem, blocks):
        view = gath.at[pl.ds(0, blocks)]
        pltpu.make_async_remote_copy(
            src_ref=view,
            dst_ref=view,
            send_sem=sem,
            recv_sem=ag_recv.at[0],
            device_id=(sibling, z),
            device_id_type=MESH,
        ).wait_send()

    gone(sib_send, ROW // 2)
    gone(ag_send, ROW // 2 - 1)


def hand_over(embed, gram, embed_out, gram_out):
    embed_out[...] = embed[...]
    gram_out[...] = gram[...]


def local(tile_values, tile_rows, tile_cols, tile_count, sketch):
    vmem = pl.BlockSpec(memory_space=pltpu.VMEM)
    hbm = pl.BlockSpec(memory_space=pltpu.HBM)
    scratch = [
        pltpu.VMEM((SLOTS + 1, TS, TS), BF16),
        pltpu.VMEM((SLOTS + 1, TS, TS), BF16),
        pltpu.VMEM((ROW, CT * KROWS, TS), BF16),
        pltpu.VMEM((CT, K, TS), BF16),
        pltpu.VMEM((2, OWN, TS), F32),
        pltpu.VMEM((KROWS, CT * TS), BF16),
        pltpu.VMEM((8, CT * TS), F32),
        pltpu.VMEM((1, SLOTS), jnp.int32),
        pltpu.VMEM((1, SLOTS), jnp.int32),
        pltpu.SMEM((1, SLOTS), jnp.int32),
        pltpu.SMEM((1, SLOTS), jnp.int32),
        pltpu.SMEM((1,), jnp.int32),
        pltpu.VMEM((8, TS), jnp.int32),
        pltpu.SMEM((8, TS), jnp.int32),
        pltpu.VMEM((CT, 8, TS), F32),
        pltpu.VMEM((U, CT // U, TS), F32),
        pltpu.VMEM((U, 8, TS), F32),
        pltpu.VMEM((8, TS), F32),
        pltpu.VMEM((Z, 8, TS), F32),
        pltpu.VMEM((Y, 16, TS), F32),
        pltpu.VMEM((U, 16, TS), F32),
        pltpu.VMEM((RT, TS, TS), F32),
        pltpu.VMEM((CT, TS), F32),
        pltpu.VMEM((2, Z, SHARE, TS), BF16),
        pltpu.VMEM((2, Z, SHARE, TS), BF16),
        pltpu.VMEM((U, GROWS, TS), BF16),
        pltpu.VMEM((U, GROWS, TS), BF16),
        pltpu.VMEM((Y, GROWS, TS), BF16),
        pltpu.VMEM((Z, GROWS, TS), BF16),
        pltpu.VMEM((U, GROWS, TS), F32),
        pltpu.SemaphoreType.DMA((4,)),
        pltpu.SemaphoreType.DMA((6,)),
        pltpu.SemaphoreType.DMA,
        pltpu.SemaphoreType.DMA,
        pltpu.SemaphoreType.DMA,
        pltpu.SemaphoreType.DMA((ROW,)),
        pltpu.SemaphoreType.DMA((10,)),
        pltpu.SemaphoreType.DMA((10, 8)),
    ]
    embed, gram = pl.pallas_call(
        kernel,
        out_shape=(
            jax.ShapeDtypeStruct((SHARE, K), F32),
            jax.ShapeDtypeStruct((K, K), F32),
        ),
        in_specs=[hbm] * 5,
        out_specs=(vmem, vmem),
        scratch_shapes=scratch,
        compiler_params=pltpu.CompilerParams(
            collective_id=0, has_side_effects=True, vmem_limit_bytes=63 * 1024 * 1024
        ),
    )(
        tile_rows.reshape(1, SLOTS),
        tile_cols.reshape(1, SLOTS),
        tile_count,
        sketch,
        tile_values,
    )
    return pl.pallas_call(
        hand_over,
        out_shape=(
            jax.ShapeDtypeStruct((SHARE, K), F32),
            jax.ShapeDtypeStruct((K, K), F32),
        ),
        in_specs=[vmem] * 2,
        out_specs=(vmem, vmem),
    )(embed, gram)


def solution(mesh):
    placed = (
        P(("row", "col"), None, None),
        P(("row", "col")),
        P(("row", "col")),
        P(("row", "col")),
        P("row", "col"),
    )
    return jax.shard_map(
        local, mesh=mesh, in_specs=placed, out_specs=(P(("row", "col"), None), P()), check_vma=False
    )
```

```python
import jax
import jax.numpy as jnp
from jax import lax
from jax.experimental import pallas as pl
from jax.experimental.pallas import tpu as pltpu
from jax.sharding import PartitionSpec as P

MESH = pl.DeviceIdType.MESH
F32 = jnp.float32
BF16 = jnp.bfloat16

TS = 128
RT = 4
CT = 64
SLOTS = 128
K = 256
X, Y, Z = 4, 8, 8
U = 2 * X
ROW = X * Y * 2
NR = ROW * RT * TS
OWN = RT * TS
SHARE = OWN // Z
KROWS = 4
GROWS = 3 * TS // U
NT_DIMS = (((1,), (1,)), ((), ()))


def wrap(value, n):
    return lax.rem(value + 4 * n, n)


def total_of(ref):
    total = ref[0].astype(F32)
    for i in range(1, ref.shape[0]):
        total = total + ref[i].astype(F32)
    return total


def each(n, f):
    def step(m, carry):
        f(m)
        return carry

    lax.fori_loop(1, n, step, 0, unroll=True)


def kernel(
    rows_h,
    cols_h,
    count_h,
    sketch_h,
    tiles,
    embed,
    gram,
    a,
    logm,
    gath,
    weights,
    acc,
    sketch,
    xf,
    rows_v,
    cols_v,
    rows_s,
    cols_s,
    count_s,
    inv_v,
    inv_s,
    colpart,
    colsrc,
    ucol,
    rowbuf,
    zrow,
    ydeg,
    udeg,
    rscale,
    cinv,
    psend,
    precv,
    gsrc,
    gu,
    gy,
    gz,
    gfin,
    tile_sem,
    in_sem,
    inv_sem,
    ag_send,
    sib_send,
    ag_recv,
    small_send,
    small_recv,
):
    row = lax.axis_index("row")
    z = lax.axis_index("col")
    core = lax.rem(row, 2)
    y = lax.rem(row // 2, Y)
    x = row // (2 * Y)
    u = 2 * x + core

    def y_peer(m):
        return wrap(y + m, Y)

    def u_peer(m):
        return wrap(u + m, U)

    def z_peer(m):
        return wrap(z + m, Z)

    def rid(xx, yy):
        return (xx * Y + yy) * 2 + core

    def y_device(v):
        return (rid(x, v), z)

    def u_device(v):
        return ((v // 2 * Y + y) * 2 + lax.rem(v, 2), z)

    def z_device(v):
        return (row, v)

    barrier = pltpu.get_barrier_semaphore()

    def greet(device):
        pl.semaphore_signal(barrier, inc=1, device_id=device, device_id_type=MESH)

    each(Y, lambda m: greet(y_device(y_peer(m))))
    each(U, lambda m: greet(u_device(u_peer(m))))
    each(Z, lambda m: greet(z_device(z_peer(m))))

    in_copies = [
        pltpu.make_async_copy(src, dst, in_sem.at[i])
        for i, (src, dst) in enumerate(
            (
                (sketch_h, sketch),
                (rows_h, rows_v),
                (cols_h, cols_v),
                (count_h, count_s),
                (rows_h, rows_s),
                (cols_h, cols_s),
            )
        )
    ]
    for copy in in_copies:
        copy.start()
    quarter = SLOTS // 4
    tile_copies = [
        pltpu.make_async_copy(
            tiles.at[pl.ds(quarter * i, quarter)],
            a.at[pl.ds(quarter * i, quarter)],
            tile_sem.at[i],
        )
        for i in range(4)
    ]
    for copy in tile_copies:
        copy.start()

    in_copies[0].wait()
    own = sketch[...].astype(F32)
    xf[pl.ds(0, KROWS), :] = own
    xf[pl.ds(KROWS, KROWS), :] = own
    low = lax.broadcasted_iota(jnp.int32, (8, TS), 0) < KROWS
    for cc in range(CT // 4):
        pieces = [xf[:, pl.ds(TS * (4 * cc + i), TS)] for i in range(4)]
        block = jnp.concatenate(
            [jnp.where(low, pieces[0], pieces[1]), jnp.where(low, pieces[2], pieces[3])], axis=0
        )
        gath[row, pl.ds(16 * cc, 16), :] = block.astype(BF16)

    for copy in in_copies[1:]:
        copy.wait()
    lane = lax.broadcasted_iota(jnp.int32, (TS, TS), 1)
    sub = lax.broadcasted_iota(jnp.int32, (TS, TS), 0)
    pos = rows_v[...] * CT + cols_v[...]
    pos = jnp.where(lane[:1] < count_s[0], pos, -1)
    pos_t = jnp.broadcast_to(pos, (TS, TS)).T
    inv_v[...] = jnp.full((8, TS), SLOTS, jnp.int32)
    for h in range(2):
        hit = pos_t == lane + TS * h
        inv_v[pl.ds(h, 1), :] = SLOTS + jnp.sum(
            jnp.where(hit, sub - SLOTS, 0), axis=0, keepdims=True
        )
    inv_copy = pltpu.make_async_copy(inv_v, inv_s, inv_sem)
    inv_copy.start()

    def slot_at(r, c):
        return inv_s[r // 2, (r % 2) * CT + c]


    a[SLOTS] = jnp.zeros((TS, TS), BF16)
    logm[SLOTS] = jnp.zeros((TS, TS), BF16)
    inv_copy.wait()
    for copy in tile_copies:
        copy.wait()
    rowbuf[...] = jnp.zeros((8, TS), F32)
    for r in range(RT):

        def add(c, total, r=r):
            tile = a[slot_at(r, c)].astype(F32)
            columns = jnp.sum(tile.reshape(TS // 8, 8, TS), axis=0)
            if r == 0:
                colpart[c] = columns
            else:
                colpart[c] += columns
            return total + tile

        total = lax.fori_loop(0, CT, add, jnp.zeros((TS, TS), F32), unroll=8)
        rowbuf[pl.ds(r, 1), :] = jnp.sum(total.T, axis=0, keepdims=True)
    colsrc[...] = jnp.sum(colpart[...], axis=1).reshape(U, CT // U, TS)

    pl.semaphore_wait(barrier, Y + U + Z - 3)

    sibling = row + 1 - 2 * core

    def block_copy(d, target):
        return pltpu.make_async_remote_copy(
            src_ref=gath.at[d],
            dst_ref=gath.at[d],
            send_sem=ag_send,
            recv_sem=ag_recv.at[d],
            device_id=(target, z),
            device_id_type=MESH,
        )

    def sibling_copy(d):
        return pltpu.make_async_remote_copy(
            src_ref=gath.at[d],
            dst_ref=gath.at[d],
            send_sem=sib_send,
            recv_sem=ag_recv.at[d],
            device_id=(sibling, z),
            device_id_type=MESH,
        )

    def arrived(d):
        sibling_copy(d).wait_recv()

    def to_sibling(d):
        sibling_copy(d).start()

    def along_x(d):
        block_copy(d, rid(wrap(x + 1, X), y)).start()
        block_copy(d, rid(wrap(x - 1, X), y)).start()

    def along_y(d, m):
        for way in (1, -1):
            if m == 0 or (way < 0 < m < Y // 2) or (way > 0 > m > 1 - Y // 2):
                block_copy(d, rid(x, y_peer(way))).start()

    def by_y(m):
        d = rid(x, y_peer(m))
        arrived(d)
        along_y(d, m)
        along_x(d)
        to_sibling(d)

    def x_pair(m):
        sign = 1 if m in (0, 1, 2, 3) else -1
        return sign, y_peer(m)

    def relay(m):
        sign, yy = x_pair(m)
        d = rid(wrap(x - sign, X), yy)
        arrived(d)
        block_copy(d, rid(wrap(x + sign, X), y)).start()
        to_sibling(d)

    def other(m):
        sign, yy = x_pair(m)
        d = rid(wrap(x + sign, X), yy)
        arrived(d)
        to_sibling(d)

    def far(m):
        d = rid(wrap(x + 2, X), y_peer(m))
        arrived(d)
        to_sibling(d)

    steps = (
        ((by_y, (1, -1)), (relay, (0,))),
        ((by_y, (2, -2)), (relay, (1, -1)), (other, (0,))),
        ((by_y, (3, -3, 4)), (relay, (2, -2)), (other, (1, -1))),
        ((relay, (3, -3, 4)), (other, (2, -2)), (far, (0, 1, -1))),
        ((other, (3, -3, 4)), (far, (2, -2))),
        ((far, (3, -3, 4)),),
    )

    def gather_step(t):
        if t == 0:
            along_x(row)
            along_y(row, 0)
            to_sibling(row)
            return
        for f, ms in steps[t - 1]:
            for m in ms:
                f(m)

    def small(phase, slot, src, dst, device):
        return pltpu.make_async_remote_copy(
            src_ref=src,
            dst_ref=dst,
            send_sem=small_send.at[phase],
            recv_sem=small_recv.at[phase, slot],
            device_id=device,
            device_id_type=MESH,
        )

    def send_y(phase, src, dst):
        each(Y, lambda m: small(phase, y, src(y_peer(m)), dst.at[y], y_device(y_peer(m))).start())

    def send_u(phase, src, dst):
        each(U, lambda m: small(phase, u, src(u_peer(m)), dst.at[u], u_device(u_peer(m))).start())

    def send_z(phase, src, dst):
        each(Z, lambda m: small(phase, z, src(z_peer(m)), dst.at[z], z_device(z_peer(m))).start())

    def recv_y(phase, dst):
        each(Y, lambda m: small(phase, y_peer(m), dst.at[y_peer(m)], dst.at[y_peer(m)], y_device(y_peer(m))).wait_recv())

    def recv_u(phase, dst):
        each(U, lambda m: small(phase, u_peer(m), dst.at[u_peer(m)], dst.at[u_peer(m)], u_device(u_peer(m))).wait_recv())

    def recv_z(phase, dst):
        each(Z, lambda m: small(phase, z_peer(m), dst.at[z_peer(m)], dst.at[z_peer(m)], z_device(z_peer(m))).wait_recv())

    def sent(phase, dst):
        view = dst.at[pl.ds(0, 7)]
        small(phase, 0, view, view, z_device(z_peer(1))).wait_send()

    send_z(0, lambda v: rowbuf, zrow)
    send_u(1, lambda v: colsrc.at[v], ucol)
    gather_step(0)
    zrow[z] = rowbuf[...]
    ucol[u] = colsrc[u]
    gather_step(1)
    recv_u(1, ucol)
    recv_z(0, zrow)
    row_sum = jnp.sum(zrow[...], axis=0)
    ydeg[y, pl.ds(0, 8), :] = jnp.sum(ucol[...], axis=0)
    ydeg[y, pl.ds(8, 8), :] = row_sum
    send_y(2, lambda v: ydeg.at[y], ydeg)
    gather_step(2)
    recv_y(2, ydeg)
    udeg[u] = jnp.sum(ydeg[...], axis=0)
    send_u(3, lambda v: udeg.at[u], udeg)
    gather_step(3)
    recv_u(3, udeg)
    cinv[...] = 1.0 / (1.0 + udeg[:, pl.ds(0, 8), :].reshape(CT, TS))
    volume = jnp.sum(jnp.sum(udeg[:, pl.ds(8, 8), :], axis=0), axis=(0, 1), keepdims=True)
    scale = volume / (1.0 + row_sum)
    for r in range(RT):
        rscale[r] = jnp.broadcast_to(scale[r : r + 1], (TS, TS)).T

    def log_step(s, carry):
        tile = a[s].astype(F32)
        ratio = tile * rscale[rows_s[0, s]] * cinv[pl.ds(cols_s[0, s], 1), :]
        logm[s] = jnp.log(jnp.maximum(ratio, 1.0)).astype(BF16)
        return carry

    lax.fori_loop(0, SLOTS // 2, log_step, 0, unroll=4)
    gather_step(4)
    lax.fori_loop(SLOTS // 2, SLOTS, log_step, 0, unroll=4)

    def arrange(xx):
        def from_sibling(i, carry):
            arrived((xx * Y + i) * 2 + 1 - core)
            return carry

        lax.fori_loop(0, Y, from_sibling, 0)

        def quad(i, carry):
            q, cc = xx * (Y // 2) + i // (CT // 4), lax.rem(i, CT // 4)
            start = pl.multiple_of(16 * cc, 16)
            parts = [gath[4 * q + j, pl.ds(start, 16), :].astype(F32) for j in range(4)]
            for half in range(2):
                f = [p[8 * half : 8 * half + 8] for p in parts]
                g = [pltpu.roll(v, 4, 0) for v in f]
                first = [jnp.where(low, f[0], g[1]), jnp.where(low, f[2], g[3])]
                second = [jnp.where(low, g[0], f[1]), jnp.where(low, g[2], f[3])]
                for j, pair in enumerate((first, second)):
                    weights[4 * cc + 2 * half + j, pl.ds(pl.multiple_of(16 * q, 16), 16), :] = (
                        jnp.concatenate(pair, axis=0).astype(BF16)
                    )
            return carry

        lax.fori_loop(0, Y // 2 * (CT // 4), quad, 0, unroll=4)

    depth = 16
    mate = x + 1 - 2 * lax.rem(x, 2)
    acc[...] = jnp.zeros((2, OWN, TS), F32)

    def products(half, top):
        def product(i, carry):
            columns = pl.ds(pl.multiple_of(half * TS, TS), TS)
            right = jnp.concatenate(
                [weights[depth * i + t, columns, :] for t in range(depth)], axis=1
            )
            left = jnp.concatenate(
                [
                    jnp.concatenate(
                        [logm[slot_at(r, depth * i + t)] for t in range(depth)], axis=1
                    )
                    for r in (2 * top, 2 * top + 1)
                ],
                axis=0,
            )
            acc[half, pl.ds(OWN // 2 * top, OWN // 2), :] += lax.dot_general(
                left, right, NT_DIMS, preferred_element_type=F32
            )
            return carry

        lax.fori_loop(0, CT // depth, product, 0)
        psend[half, pl.ds(Z // 2 * top, Z // 2)] = (
            acc[half, pl.ds(OWN // 2 * top, OWN // 2), :]
            .reshape(Z // 2, SHARE, TS)
            .astype(BF16)
        )

    def scatter(phase, half, top):
        for i in range(Z // 2):
            v = Z // 2 * top + i

            @pl.when(z != v)
            def _(v=v):
                small(phase, z, psend.at[half, v], precv.at[half, z], z_device(v)).start()

    arrange(x)
    gather_step(5)
    arrange(mate)
    early = x // 2
    products(early, 0)
    scatter(4, early, 0)
    gather_step(6)
    products(early, 1)
    scatter(4, early, 1)
    arrange(wrap(x + 2, X))
    arrange(wrap(mate + 2, X))
    for top in range(2):
        products(1 - early, top)
        scatter(9, 1 - early, top)
    for half in range(2):
        precv[half, z] = jnp.zeros((SHARE, TS), BF16)
    recv_z(4, precv.at[early])
    recv_z(9, precv.at[1 - early])
    parts = []
    for half in range(2):
        part = acc[half, pl.ds(pl.multiple_of(z * SHARE, SHARE), SHARE), :]
        for i in range(Z):
            part = part + precv[half, i].astype(F32)
        embed[:, pl.ds(TS * half, TS)] = part
        parts.append(part)
    result = jnp.concatenate(parts, axis=1)

    local_gram = lax.dot_general(
        result,
        result,
        (((0,), (0,)), ((), ())),
        precision=lax.Precision.HIGHEST,
        preferred_element_type=F32,
    ) * (1.0 / NR)
    gsrc[...] = (
        jnp.concatenate([local_gram[:TS, :TS], local_gram[:, TS:]], axis=0)
        .reshape(U, GROWS, TS)
        .astype(BF16)
    )
    send_u(5, lambda v: gsrc.at[v], gu)
    gu[u] = gsrc[u]
    recv_u(5, gu)
    gy[y] = total_of(gu).astype(BF16)
    send_y(6, lambda v: gy.at[y], gy)
    recv_y(6, gy)
    gz[z] = total_of(gy).astype(BF16)
    send_z(7, lambda v: gz.at[z], gz)
    recv_z(7, gz)
    gfin[u] = total_of(gz)
    send_u(8, lambda v: gfin.at[u], gfin)
    recv_u(8, gfin)
    packed = gfin[...].reshape(3 * TS, TS)
    gram[pl.ds(0, TS), pl.ds(0, TS)] = packed[:TS]
    gram[:, pl.ds(TS, TS)] = packed[TS:]
    gram[pl.ds(TS, TS), pl.ds(0, TS)] = packed[TS : 2 * TS].T

    sent(0, zrow)
    sent(1, ucol)
    sent(2, ydeg)
    sent(3, udeg)
    sent(4, precv.at[0])
    sent(9, precv.at[1])
    sent(5, gu)
    sent(6, gy)
    sent(7, gz)
    sent(8, gfin)
    def gone(sem, blocks):
        view = gath.at[pl.ds(0, blocks)]
        pltpu.make_async_remote_copy(
            src_ref=view,
            dst_ref=view,
            send_sem=sem,
            recv_sem=ag_recv.at[0],
            device_id=(sibling, z),
            device_id_type=MESH,
        ).wait_send()

    gone(sib_send, ROW // 2)
    gone(ag_send, ROW // 2 - 1)


def hand_over(embed, gram, embed_out, gram_out):
    embed_out[...] = embed[...]
    gram_out[...] = gram[...]


def local(tile_values, tile_rows, tile_cols, tile_count, sketch):
    vmem = pl.BlockSpec(memory_space=pltpu.VMEM)
    hbm = pl.BlockSpec(memory_space=pltpu.HBM)
    scratch = [
        pltpu.VMEM((SLOTS + 1, TS, TS), BF16),
        pltpu.VMEM((SLOTS + 1, TS, TS), BF16),
        pltpu.VMEM((ROW, CT * KROWS, TS), BF16),
        pltpu.VMEM((CT, K, TS), BF16),
        pltpu.VMEM((2, OWN, TS), F32),
        pltpu.VMEM((KROWS, CT * TS), BF16),
        pltpu.VMEM((8, CT * TS), F32),
        pltpu.VMEM((1, SLOTS), jnp.int32),
        pltpu.VMEM((1, SLOTS), jnp.int32),
        pltpu.SMEM((1, SLOTS), jnp.int32),
        pltpu.SMEM((1, SLOTS), jnp.int32),
        pltpu.SMEM((1,), jnp.int32),
        pltpu.VMEM((8, TS), jnp.int32),
        pltpu.SMEM((8, TS), jnp.int32),
        pltpu.VMEM((CT, 8, TS), F32),
        pltpu.VMEM((U, CT // U, TS), F32),
        pltpu.VMEM((U, 8, TS), F32),
        pltpu.VMEM((8, TS), F32),
        pltpu.VMEM((Z, 8, TS), F32),
        pltpu.VMEM((Y, 16, TS), F32),
        pltpu.VMEM((U, 16, TS), F32),
        pltpu.VMEM((RT, TS, TS), F32),
        pltpu.VMEM((CT, TS), F32),
        pltpu.VMEM((2, Z, SHARE, TS), BF16),
        pltpu.VMEM((2, Z, SHARE, TS), BF16),
        pltpu.VMEM((U, GROWS, TS), BF16),
        pltpu.VMEM((U, GROWS, TS), BF16),
        pltpu.VMEM((Y, GROWS, TS), BF16),
        pltpu.VMEM((Z, GROWS, TS), BF16),
        pltpu.VMEM((U, GROWS, TS), F32),
        pltpu.SemaphoreType.DMA((4,)),
        pltpu.SemaphoreType.DMA((6,)),
        pltpu.SemaphoreType.DMA,
        pltpu.SemaphoreType.DMA,
        pltpu.SemaphoreType.DMA,
        pltpu.SemaphoreType.DMA((ROW,)),
        pltpu.SemaphoreType.DMA((10,)),
        pltpu.SemaphoreType.DMA((10, 8)),
    ]
    embed, gram = pl.pallas_call(
        kernel,
        out_shape=(
            jax.ShapeDtypeStruct((SHARE, K), F32),
            jax.ShapeDtypeStruct((K, K), F32),
        ),
        in_specs=[hbm] * 5,
        out_specs=(vmem, vmem),
        scratch_shapes=scratch,
        compiler_params=pltpu.CompilerParams(
            collective_id=0, has_side_effects=True, vmem_limit_bytes=63 * 1024 * 1024
        ),
    )(
        tile_rows.reshape(1, SLOTS),
        tile_cols.reshape(1, SLOTS),
        tile_count,
        sketch,
        tile_values,
    )
    return pl.pallas_call(
        hand_over,
        out_shape=(
            jax.ShapeDtypeStruct((SHARE, K), F32),
            jax.ShapeDtypeStruct((K, K), F32),
        ),
        in_specs=[vmem] * 2,
        out_specs=(vmem, vmem),
    )(embed, gram)


def solution(mesh):
    placed = (
        P(("row", "col"), None, None),
        P(("row", "col")),
        P(("row", "col")),
        P(("row", "col")),
        P("row", "col"),
    )
    return jax.shard_map(
        local, mesh=mesh, in_specs=placed, out_specs=(P(("row", "col"), None), P()), check_vma=False
    )
```

```python
import jax
import jax.numpy as jnp
from jax import lax
from jax.experimental import pallas as pl
from jax.experimental.pallas import tpu as pltpu
from jax.sharding import PartitionSpec as P

MESH = pl.DeviceIdType.MESH
F32 = jnp.float32
BF16 = jnp.bfloat16

TS = 128
RT = 4
CT = 64
SLOTS = 128
K = 256
X, Y, Z = 4, 8, 8
U = 2 * X
ROW = X * Y * 2
NR = ROW * RT * TS
OWN = RT * TS
SHARE = OWN // Z
KROWS = 4
GROWS = 3 * TS // U
NT_DIMS = (((1,), (1,)), ((), ()))


def wrap(value, n):
    return lax.rem(value + 4 * n, n)


def total_of(ref):
    total = ref[0].astype(F32)
    for i in range(1, ref.shape[0]):
        total = total + ref[i].astype(F32)
    return total


def each(n, f):
    def step(m, carry):
        f(m)
        return carry

    lax.fori_loop(1, n, step, 0, unroll=True)


def kernel(
    rows_h,
    cols_h,
    count_h,
    sketch_h,
    tiles,
    embed,
    blocks,
    a,
    logm,
    gath,
    weights,
    acc,
    sketch,
    xf,
    rows_v,
    cols_v,
    rows_s,
    cols_s,
    count_s,
    inv_v,
    inv_s,
    colpart,
    colsrc,
    ucol,
    rowbuf,
    zrow,
    ydeg,
    udeg,
    rscale,
    cinv,
    psend,
    precv,
    gsrc,
    gu,
    gy,
    gz,
    gfin,
    tile_sem,
    in_sem,
    inv_sem,
    ag_send,
    sib_send,
    ag_recv,
    small_send,
    small_recv,
):
    row = lax.axis_index("row")
    z = lax.axis_index("col")
    core = lax.rem(row, 2)
    y = lax.rem(row // 2, Y)
    x = row // (2 * Y)
    u = 2 * x + core

    def y_peer(m):
        return wrap(y + m, Y)

    def u_peer(m):
        return wrap(u + m, U)

    def z_peer(m):
        return wrap(z + m, Z)

    def rid(xx, yy):
        return (xx * Y + yy) * 2 + core

    def y_device(v):
        return (rid(x, v), z)

    def u_device(v):
        return ((v // 2 * Y + y) * 2 + lax.rem(v, 2), z)

    def z_device(v):
        return (row, v)

    barrier = pltpu.get_barrier_semaphore()

    def greet(device):
        pl.semaphore_signal(barrier, inc=1, device_id=device, device_id_type=MESH)

    each(Y, lambda m: greet(y_device(y_peer(m))))
    each(U, lambda m: greet(u_device(u_peer(m))))
    each(Z, lambda m: greet(z_device(z_peer(m))))

    in_copies = [
        pltpu.make_async_copy(src, dst, in_sem.at[i])
        for i, (src, dst) in enumerate(
            (
                (sketch_h, sketch),
                (rows_h, rows_v),
                (cols_h, cols_v),
                (count_h, count_s),
                (rows_h, rows_s),
                (cols_h, cols_s),
            )
        )
    ]
    for copy in in_copies:
        copy.start()
    quarter = SLOTS // 4
    tile_copies = [
        pltpu.make_async_copy(
            tiles.at[pl.ds(quarter * i, quarter)],
            a.at[pl.ds(quarter * i, quarter)],
            tile_sem.at[i],
        )
        for i in range(4)
    ]
    for copy in tile_copies:
        copy.start()

    in_copies[0].wait()
    own = sketch[...].astype(F32)
    xf[pl.ds(0, KROWS), :] = own
    xf[pl.ds(KROWS, KROWS), :] = own
    low = lax.broadcasted_iota(jnp.int32, (8, TS), 0) < KROWS
    for cc in range(CT // 4):
        pieces = [xf[:, pl.ds(TS * (4 * cc + i), TS)] for i in range(4)]
        block = jnp.concatenate(
            [jnp.where(low, pieces[0], pieces[1]), jnp.where(low, pieces[2], pieces[3])], axis=0
        )
        gath[row, pl.ds(16 * cc, 16), :] = block.astype(BF16)

    for copy in in_copies[1:]:
        copy.wait()
    lane = lax.broadcasted_iota(jnp.int32, (TS, TS), 1)
    sub = lax.broadcasted_iota(jnp.int32, (TS, TS), 0)
    pos = rows_v[...] * CT + cols_v[...]
    pos = jnp.where(lane[:1] < count_s[0], pos, -1)
    pos_t = jnp.broadcast_to(pos, (TS, TS)).T
    inv_v[...] = jnp.full((8, TS), SLOTS, jnp.int32)
    for h in range(2):
        hit = pos_t == lane + TS * h
        inv_v[pl.ds(h, 1), :] = SLOTS + jnp.sum(
            jnp.where(hit, sub - SLOTS, 0), axis=0, keepdims=True
        )
    inv_copy = pltpu.make_async_copy(inv_v, inv_s, inv_sem)
    inv_copy.start()

    def slot_at(r, c):
        return inv_s[r // 2, (r % 2) * CT + c]


    a[SLOTS] = jnp.zeros((TS, TS), BF16)
    logm[SLOTS] = jnp.zeros((TS, TS), BF16)
    inv_copy.wait()
    for copy in tile_copies:
        copy.wait()
    rowbuf[...] = jnp.zeros((8, TS), F32)
    for r in range(RT):

        def add(c, total, r=r):
            tile = a[slot_at(r, c)].astype(F32)
            columns = jnp.sum(tile.reshape(TS // 8, 8, TS), axis=0)
            if r == 0:
                colpart[c] = columns
            else:
                colpart[c] += columns
            return total + tile

        total = lax.fori_loop(0, CT, add, jnp.zeros((TS, TS), F32), unroll=8)
        rowbuf[pl.ds(r, 1), :] = jnp.sum(total.T, axis=0, keepdims=True)
    colsrc[...] = jnp.sum(colpart[...], axis=1).reshape(U, CT // U, TS)

    pl.semaphore_wait(barrier, Y + U + Z - 3)

    sibling = row + 1 - 2 * core

    def block_copy(d, target):
        return pltpu.make_async_remote_copy(
            src_ref=gath.at[d],
            dst_ref=gath.at[d],
            send_sem=ag_send,
            recv_sem=ag_recv.at[d],
            device_id=(target, z),
            device_id_type=MESH,
        )

    def sibling_copy(d):
        return pltpu.make_async_remote_copy(
            src_ref=gath.at[d],
            dst_ref=gath.at[d],
            send_sem=sib_send,
            recv_sem=ag_recv.at[d],
            device_id=(sibling, z),
            device_id_type=MESH,
        )

    def arrived(d):
        sibling_copy(d).wait_recv()

    def to_sibling(d):
        sibling_copy(d).start()

    def along_x(d):
        block_copy(d, rid(wrap(x + 1, X), y)).start()
        block_copy(d, rid(wrap(x - 1, X), y)).start()

    def along_y(d, m):
        for way in (1, -1):
            if m == 0 or (way < 0 < m < Y // 2) or (way > 0 > m > 1 - Y // 2):
                block_copy(d, rid(x, y_peer(way))).start()

    def by_y(m):
        d = rid(x, y_peer(m))
        arrived(d)
        along_y(d, m)
        along_x(d)
        to_sibling(d)

    def x_pair(m):
        sign = 1 if m in (0, 1, 2, 3) else -1
        return sign, y_peer(m)

    def relay(m):
        sign, yy = x_pair(m)
        d = rid(wrap(x - sign, X), yy)
        arrived(d)
        block_copy(d, rid(wrap(x + sign, X), y)).start()
        to_sibling(d)

    def other(m):
        sign, yy = x_pair(m)
        d = rid(wrap(x + sign, X), yy)
        arrived(d)
        to_sibling(d)

    def far(m):
        d = rid(wrap(x + 2, X), y_peer(m))
        arrived(d)
        to_sibling(d)

    steps = (
        ((by_y, (1, -1)), (relay, (0,))),
        ((by_y, (2, -2)), (relay, (1, -1)), (other, (0,))),
        ((by_y, (3, -3, 4)), (relay, (2, -2)), (other, (1, -1))),
        ((relay, (3, -3, 4)), (other, (2, -2)), (far, (0, 1, -1))),
        ((other, (3, -3, 4)), (far, (2, -2))),
        ((far, (3, -3, 4)),),
    )

    def gather_step(t):
        if t == 0:
            along_x(row)
            along_y(row, 0)
            to_sibling(row)
            return
        for f, ms in steps[t - 1]:
            for m in ms:
                f(m)

    def small(phase, slot, src, dst, device):
        return pltpu.make_async_remote_copy(
            src_ref=src,
            dst_ref=dst,
            send_sem=small_send.at[phase],
            recv_sem=small_recv.at[phase, slot],
            device_id=device,
            device_id_type=MESH,
        )

    def send_y(phase, src, dst):
        each(Y, lambda m: small(phase, y, src(y_peer(m)), dst.at[y], y_device(y_peer(m))).start())

    def send_u(phase, src, dst):
        each(U, lambda m: small(phase, u, src(u_peer(m)), dst.at[u], u_device(u_peer(m))).start())

    def send_z(phase, src, dst):
        each(Z, lambda m: small(phase, z, src(z_peer(m)), dst.at[z], z_device(z_peer(m))).start())

    def recv_y(phase, dst):
        each(Y, lambda m: small(phase, y_peer(m), dst.at[y_peer(m)], dst.at[y_peer(m)], y_device(y_peer(m))).wait_recv())

    def recv_u(phase, dst):
        each(U, lambda m: small(phase, u_peer(m), dst.at[u_peer(m)], dst.at[u_peer(m)], u_device(u_peer(m))).wait_recv())

    def recv_z(phase, dst):
        each(Z, lambda m: small(phase, z_peer(m), dst.at[z_peer(m)], dst.at[z_peer(m)], z_device(z_peer(m))).wait_recv())

    def sent(phase, dst):
        view = dst.at[pl.ds(0, 7)]
        small(phase, 0, view, view, z_device(z_peer(1))).wait_send()

    send_z(0, lambda v: rowbuf, zrow)
    send_u(1, lambda v: colsrc.at[v], ucol)
    gather_step(0)
    zrow[z] = rowbuf[...]
    ucol[u] = colsrc[u]
    gather_step(1)
    recv_u(1, ucol)
    recv_z(0, zrow)
    row_sum = jnp.sum(zrow[...], axis=0)
    ydeg[y, pl.ds(0, 8), :] = jnp.sum(ucol[...], axis=0)
    ydeg[y, pl.ds(8, 8), :] = row_sum
    send_y(2, lambda v: ydeg.at[y], ydeg)
    gather_step(2)
    recv_y(2, ydeg)
    udeg[u] = jnp.sum(ydeg[...], axis=0)
    send_u(3, lambda v: udeg.at[u], udeg)
    gather_step(3)
    recv_u(3, udeg)
    cinv[...] = 1.0 / (1.0 + udeg[:, pl.ds(0, 8), :].reshape(CT, TS))
    volume = jnp.sum(jnp.sum(udeg[:, pl.ds(8, 8), :], axis=0), axis=(0, 1), keepdims=True)
    scale = volume / (1.0 + row_sum)
    for r in range(RT):
        rscale[r] = jnp.broadcast_to(scale[r : r + 1], (TS, TS)).T

    def log_step(s, carry):
        tile = a[s].astype(F32)
        ratio = tile * rscale[rows_s[0, s]] * cinv[pl.ds(cols_s[0, s], 1), :]
        logm[s] = jnp.log(jnp.maximum(ratio, 1.0)).astype(BF16)
        return carry

    lax.fori_loop(0, SLOTS // 2, log_step, 0, unroll=4)
    gather_step(4)
    lax.fori_loop(SLOTS // 2, SLOTS, log_step, 0, unroll=4)

    def arrange(xx):
        def from_sibling(i, carry):
            arrived((xx * Y + i) * 2 + 1 - core)
            return carry

        lax.fori_loop(0, Y, from_sibling, 0)

        def quad(i, carry):
            q, cc = xx * (Y // 2) + i // (CT // 4), lax.rem(i, CT // 4)
            start = pl.multiple_of(16 * cc, 16)
            parts = [gath[4 * q + j, pl.ds(start, 16), :].astype(F32) for j in range(4)]
            for half in range(2):
                f = [p[8 * half : 8 * half + 8] for p in parts]
                g = [pltpu.roll(v, 4, 0) for v in f]
                first = [jnp.where(low, f[0], g[1]), jnp.where(low, f[2], g[3])]
                second = [jnp.where(low, g[0], f[1]), jnp.where(low, g[2], f[3])]
                for j, pair in enumerate((first, second)):
                    weights[4 * cc + 2 * half + j, pl.ds(pl.multiple_of(16 * q, 16), 16), :] = (
                        jnp.concatenate(pair, axis=0).astype(BF16)
                    )
            return carry

        lax.fori_loop(0, Y // 2 * (CT // 4), quad, 0, unroll=4)

    depth = 16
    mate = x + 1 - 2 * lax.rem(x, 2)
    acc[...] = jnp.zeros((2, OWN, TS), F32)

    def products(half, top):
        def product(i, carry):
            columns = pl.ds(pl.multiple_of(half * TS, TS), TS)
            right = jnp.concatenate(
                [weights[depth * i + t, columns, :] for t in range(depth)], axis=1
            )
            left = jnp.concatenate(
                [
                    jnp.concatenate(
                        [logm[slot_at(r, depth * i + t)] for t in range(depth)], axis=1
                    )
                    for r in (2 * top, 2 * top + 1)
                ],
                axis=0,
            )
            acc[half, pl.ds(OWN // 2 * top, OWN // 2), :] += lax.dot_general(
                left, right, NT_DIMS, preferred_element_type=F32
            )
            return carry

        lax.fori_loop(0, CT // depth, product, 0)
        psend[half, pl.ds(Z // 2 * top, Z // 2)] = (
            acc[half, pl.ds(OWN // 2 * top, OWN // 2), :]
            .reshape(Z // 2, SHARE, TS)
            .astype(BF16)
        )

    def scatter(phase, half, top):
        for i in range(Z // 2):
            v = Z // 2 * top + i

            @pl.when(z != v)
            def _(v=v):
                small(phase, z, psend.at[half, v], precv.at[half, z], z_device(v)).start()

    arrange(x)
    gather_step(5)
    arrange(mate)
    early = x // 2
    products(early, 0)
    scatter(4, early, 0)
    gather_step(6)
    products(early, 1)
    scatter(4, early, 1)
    arrange(wrap(x + 2, X))
    arrange(wrap(mate + 2, X))
    for top in range(2):
        products(1 - early, top)
        scatter(9, 1 - early, top)
    for half in range(2):
        precv[half, z] = jnp.zeros((SHARE, TS), BF16)
    recv_z(4, precv.at[early])
    recv_z(9, precv.at[1 - early])
    parts = []
    for half in range(2):
        part = acc[half, pl.ds(pl.multiple_of(z * SHARE, SHARE), SHARE), :]
        for i in range(Z):
            part = part + precv[half, i].astype(F32)
        embed[:, pl.ds(TS * half, TS)] = part
        parts.append(part)
    result = jnp.concatenate(parts, axis=1)

    local_gram = lax.dot_general(
        result,
        result,
        (((0,), (0,)), ((), ())),
        precision=lax.Precision.HIGHEST,
        preferred_element_type=F32,
    ) * (1.0 / NR)
    gsrc[...] = (
        jnp.concatenate([local_gram[:TS, :TS], local_gram[:, TS:]], axis=0)
        .reshape(U, GROWS, TS)
        .astype(BF16)
    )
    send_u(5, lambda v: gsrc.at[v], gu)
    gu[u] = gsrc[u]
    recv_u(5, gu)
    gy[y] = total_of(gu).astype(BF16)
    send_y(6, lambda v: gy.at[y], gy)
    recv_y(6, gy)
    gz[z] = total_of(gy).astype(BF16)
    send_z(7, lambda v: gz.at[z], gz)
    recv_z(7, gz)
    gfin[u] = total_of(gz)
    send_u(8, lambda v: gfin.at[u], gfin)
    recv_u(8, gfin)
    blocks[...] = gfin[...].reshape(3 * TS, TS)

    sent(0, zrow)
    sent(1, ucol)
    sent(2, ydeg)
    sent(3, udeg)
    sent(4, precv.at[0])
    sent(9, precv.at[1])
    sent(5, gu)
    sent(6, gy)
    sent(7, gz)
    sent(8, gfin)
    def gone(sem, blocks):
        view = gath.at[pl.ds(0, blocks)]
        pltpu.make_async_remote_copy(
            src_ref=view,
            dst_ref=view,
            send_sem=sem,
            recv_sem=ag_recv.at[0],
            device_id=(sibling, z),
            device_id_type=MESH,
        ).wait_send()

    gone(sib_send, ROW // 2)
    gone(ag_send, ROW // 2 - 1)


def hand_over(embed, blocks, embed_out, gram_out):
    embed_out[...] = embed[...]
    gram_out[pl.ds(0, TS), pl.ds(0, TS)] = blocks[pl.ds(0, TS), :]
    gram_out[:, pl.ds(TS, TS)] = blocks[pl.ds(TS, 2 * TS), :]
    gram_out[pl.ds(TS, TS), pl.ds(0, TS)] = blocks[pl.ds(TS, TS), :].T


def local(tile_values, tile_rows, tile_cols, tile_count, sketch):
    vmem = pl.BlockSpec(memory_space=pltpu.VMEM)
    hbm = pl.BlockSpec(memory_space=pltpu.HBM)
    scratch = [
        pltpu.VMEM((SLOTS + 1, TS, TS), BF16),
        pltpu.VMEM((SLOTS + 1, TS, TS), BF16),
        pltpu.VMEM((ROW, CT * KROWS, TS), BF16),
        pltpu.VMEM((CT, K, TS), BF16),
        pltpu.VMEM((2, OWN, TS), F32),
        pltpu.VMEM((KROWS, CT * TS), BF16),
        pltpu.VMEM((8, CT * TS), F32),
        pltpu.VMEM((1, SLOTS), jnp.int32),
        pltpu.VMEM((1, SLOTS), jnp.int32),
        pltpu.SMEM((1, SLOTS), jnp.int32),
        pltpu.SMEM((1, SLOTS), jnp.int32),
        pltpu.SMEM((1,), jnp.int32),
        pltpu.VMEM((8, TS), jnp.int32),
        pltpu.SMEM((8, TS), jnp.int32),
        pltpu.VMEM((CT, 8, TS), F32),
        pltpu.VMEM((U, CT // U, TS), F32),
        pltpu.VMEM((U, 8, TS), F32),
        pltpu.VMEM((8, TS), F32),
        pltpu.VMEM((Z, 8, TS), F32),
        pltpu.VMEM((Y, 16, TS), F32),
        pltpu.VMEM((U, 16, TS), F32),
        pltpu.VMEM((RT, TS, TS), F32),
        pltpu.VMEM((CT, TS), F32),
        pltpu.VMEM((2, Z, SHARE, TS), BF16),
        pltpu.VMEM((2, Z, SHARE, TS), BF16),
        pltpu.VMEM((U, GROWS, TS), BF16),
        pltpu.VMEM((U, GROWS, TS), BF16),
        pltpu.VMEM((Y, GROWS, TS), BF16),
        pltpu.VMEM((Z, GROWS, TS), BF16),
        pltpu.VMEM((U, GROWS, TS), F32),
        pltpu.SemaphoreType.DMA((4,)),
        pltpu.SemaphoreType.DMA((6,)),
        pltpu.SemaphoreType.DMA,
        pltpu.SemaphoreType.DMA,
        pltpu.SemaphoreType.DMA,
        pltpu.SemaphoreType.DMA((ROW,)),
        pltpu.SemaphoreType.DMA((10,)),
        pltpu.SemaphoreType.DMA((10, 8)),
    ]
    embed, blocks = pl.pallas_call(
        kernel,
        out_shape=(
            jax.ShapeDtypeStruct((SHARE, K), F32),
            jax.ShapeDtypeStruct((3 * TS, TS), F32),
        ),
        in_specs=[hbm] * 5,
        out_specs=(vmem, vmem),
        scratch_shapes=scratch,
        compiler_params=pltpu.CompilerParams(
            collective_id=0, has_side_effects=True, vmem_limit_bytes=63 * 1024 * 1024
        ),
    )(
        tile_rows.reshape(1, SLOTS),
        tile_cols.reshape(1, SLOTS),
        tile_count,
        sketch,
        tile_values,
    )
    return pl.pallas_call(
        hand_over,
        out_shape=(
            jax.ShapeDtypeStruct((SHARE, K), F32),
            jax.ShapeDtypeStruct((K, K), F32),
        ),
        in_specs=[vmem] * 2,
        out_specs=(vmem, vmem),
    )(embed, blocks)


def solution(mesh):
    placed = (
        P(("row", "col"), None, None),
        P(("row", "col")),
        P(("row", "col")),
        P(("row", "col")),
        P("row", "col"),
    )
    return jax.shard_map(
        local, mesh=mesh, in_specs=placed, out_specs=(P(("row", "col"), None), P()), check_vma=False
    )
```
